256 devices in a mesh: pair: 64 (over x, z, core), aux: 4 (over y).
Axes of the slice: x: 4, y: 4, z: 8, core: 2. Of those that a mesh axis runs over, the one named last changes fastest.
Arguments:
- three_index: bfloat16 [256, 32, 32, 2048], P('pair', None, None, 'aux'), may hold values from -6 to 6
- occ_blocks: bfloat16 [64, 3, 32, 32], P('pair'), may hold values from -0.625 to 0.625
- virt_blocks: bfloat16 [64, 7, 32, 32], P('pair'), may hold values from -0.5 to 0.5
- tile_shift: int32 [64, 4], replicated, may hold values from 0 to 3, each once within a row
- tile_count: int32 [64], replicated, may hold values from 1 to 4, 128 in all
- block_owner: int32 [64], replicated, may hold values from 0 to 63, each once
Outputs:
- polarizability: float32 [2048, 2048], P('pair', 'aux')
The draws below stay inside these ranges and needn't reach their ends.
Inputs may be any that keep to these rules, and one draw needn't show every extreme that they name: `tile_shift`: each row holds every offset once. `tile_count`: the counts sum to 128 and the largest is 4; slots at or beyond a device's count are not used. `block_owner`: every device owns exactly one block row.
All inputs are finite; a program needn't handle non-finite values.
Results may differ from the reference program's by a relative error of at most 0.0041.
Values may be sent and summed in bfloat16 or wider, within the bound.
A program may use at most 128 MiB of HBM per device.

```python
import math
import jax
import jax.numpy as jnp
import numpy as np
from jax import lax

TB = 32
NAUX = 2048
TPD = 2
SLOTS = 4
NBLK = 64


def shard_levels(own_key, extent, shards, low, largest):
    def one(position, parts):
        heights = jax.random.uniform(jax.random.fold_in(jax.random.fold_in(own_key, 6), position), (parts,), jnp.float32, low / len(shards), largest / len(shards))
        return jnp.repeat(jnp.exp(heights), extent[position] // parts).reshape((-1,) + (1,) * (len(extent) - position - 1))

    factor_of = one(*shards[0])
    for cut in shards[1:]:
        factor_of = factor_of * one(*cut)
    return factor_of


def length_profile(count, total, bound, skew):
    weights = [(1 << 20) // math.isqrt(standing ** skew) + 1 for standing in range(2, count + 1)]
    spare, counts = total - bound - (count - 1), [1] * (count - 1)
    while spare > 0:
        free = [i for i in range(count - 1) if counts[i] < bound]
        mass, budget = sum([weights[i] for i in free]), spare
        for i in free:
            extra = min(bound - counts[i], max(1, budget * weights[i] // mass), spare)
            counts[i] = counts[i] + extra
            spare = spare - extra
    return np.array([bound] + counts)


def uneven(own_key, count, total, limit, skew):
    if count == 2:
        one = jax.random.randint(own_key, (), max(1, total - limit), min(limit, total - 1) + 1)
        return jnp.stack([one, total - one])
    tallies = jnp.asarray(length_profile(count, total, limit, skew), jnp.int32)
    pairs = (count - 1) // 2
    source_of, taker = tallies[1:1 + 2 * pairs:2], tallies[2:2 + 2 * pairs:2]
    margin = jnp.minimum(source_of - 1, limit - taker)
    moved = jax.random.randint(jax.random.fold_in(own_key, 1), (pairs,), 0, 1 << 20) % (margin + 1)
    tallies = tallies.at[1:1 + 2 * pairs:2].set(source_of - moved).at[2:2 + 2 * pairs:2].set(taker + moved)
    return tallies[jax.random.permutation(jax.random.fold_in(own_key, 2), count)]


def noise(rng, extent, spread, reach, shards=(), kind=jnp.bfloat16):
    entries = jax.random.normal(rng, extent, jnp.float32) * spread
    if len(shards) > 0:
        entries = shard_levels(rng, extent, shards, -0.22, 0.18) * entries
    return jnp.clip(entries, min=-reach, max=reach).astype(kind)


def setup_inputs(seed: int = 0) -> dict:
    streams_of = jax.random.split(jax.random.key(seed), 7)
    return {
        "three_index": noise(streams_of[0], (NBLK * SLOTS, TB, TB, NAUX), 1.0, 6.0, ((0, 64), (3, 4))),
        "occ_blocks": noise(streams_of[1], (NBLK, 3, TB, TB), (3 * TB) ** -0.5, 0.625, ((0, 64),)),
        "virt_blocks": noise(streams_of[2], (NBLK, 2 * SLOTS - 1, TB, TB), (SLOTS * TB) ** -0.5, 0.5, ((0, 64),)),
        "tile_shift": jax.vmap(lambda own: jax.random.permutation(own, SLOTS))(jax.random.split(streams_of[3], NBLK)).reshape((NBLK, SLOTS)).astype(jnp.int32),
        "tile_count": uneven(streams_of[4], NBLK, NBLK * TPD, SLOTS, 2).astype(jnp.int32),
        "block_owner": jax.random.permutation(streams_of[5], NBLK).astype(jnp.int32),
    }


def tile_tables(tile_shift, tile_count, block_owner):
    block_count = block_owner.shape[0]
    slot_count = tile_shift.shape[1]
    devices = tile_count.shape[0]
    device_ids = jnp.arange(devices, dtype=jnp.int32)
    block_ids = jnp.arange(block_count, dtype=jnp.int32)
    row_block = lax.optimization_barrier(jnp.sum(jnp.where(block_owner[None, :] == device_ids[:, None], block_ids[None, :], 0), axis=1)).astype(jnp.int32)
    col_block = ((row_block[:, None] + tile_shift - slot_count // 2) % block_count).astype(jnp.int32)
    slot_ids = jnp.arange(slot_count, dtype=jnp.int32)
    tile_live = slot_ids[None, :] < tile_count[:, None]
    return (row_block, col_block, tile_live)

def virtual_pairs(virt_blocks, col_block, tile_live):
    block_count = virt_blocks.shape[0]
    centre = (virt_blocks.shape[1] - 1) // 2
    offset = (col_block[:, None, :] - col_block[:, :, None]) % block_count
    offset = (jnp.where(offset > block_count // 2, offset - block_count, offset) + centre).astype(jnp.int32)
    chosen = virt_blocks[col_block[:, :, None], offset]
    return jnp.where(tile_live[:, None, :, None, None], chosen, jnp.zeros((), virt_blocks.dtype))

def occupied_sources(row_block, col_block, tile_live, block_owner):
    block_count = block_owner.shape[0]
    slot_count = col_block.shape[1]
    slot_ids = jnp.arange(slot_count, dtype=jnp.int32)
    source_list = []
    found_list = []
    for neighbour in range(3):
        near_block = ((row_block + neighbour - 1) % block_count).astype(jnp.int32)
        owner_device = block_owner[near_block]
        near_cols = col_block[owner_device]
        near_live = tile_live[owner_device]
        matches = (near_cols[:, None, :] == col_block[:, :, None]) & near_live[:, None, :]
        present = jnp.any(matches, axis=2) & tile_live
        position_in = lax.optimization_barrier(jnp.sum(jnp.where(matches, slot_ids[None, None, :], 0), axis=2)).astype(jnp.int32)
        source_list.append((owner_device[:, None] * slot_count + position_in).astype(jnp.int32))
        found_list.append(present)
    return (jnp.stack(source_list, axis=2), jnp.stack(found_list, axis=2))

def balanced_index(tile_count, slot_count, live_total):
    devices = tile_count.shape[0]
    block_ends = jnp.cumsum(tile_count, dtype=jnp.int32)
    starts = (block_ends - tile_count).astype(jnp.int32)
    rank_ids = jnp.arange(live_total, dtype=jnp.int32)
    owner_device = lax.optimization_barrier(jnp.sum((block_ends[None, :] <= rank_ids[:, None]).astype(jnp.int32), axis=1)).astype(jnp.int32)
    device_ids = jnp.arange(devices, dtype=jnp.int32)
    first_rank = lax.optimization_barrier(jnp.sum(jnp.where(device_ids[None, :] == owner_device[:, None], starts[None, :], 0), axis=1)).astype(jnp.int32)
    return (owner_device * slot_count + rank_ids - first_rank).astype(jnp.int32)

def reference(three_index, occ_blocks, virt_blocks, tile_shift, tile_count, block_owner):
    row_block, col_block, tile_live = tile_tables(tile_shift, tile_count, block_owner)
    virt_pairs = virtual_pairs(virt_blocks, col_block, tile_live).astype(jnp.float32)
    sources, valid = occupied_sources(row_block, col_block, tile_live, block_owner)
    tile_total = NBLK * SLOTS
    live_total = NBLK * TPD
    picked = balanced_index(tile_count, SLOTS, live_total)
    sources = sources.reshape(tile_total, 3)[picked]
    valid = valid.reshape(tile_total, 3)[picked]
    occ_rows = occ_blocks[jnp.repeat(row_block, SLOTS)][picked]
    occ_rows = jnp.where(valid[:, :, None, None], occ_rows, jnp.zeros((), occ_blocks.dtype)).astype(jnp.float32)
    tile_grid = three_index.reshape(NBLK, SLOTS, TB, TB, NAUX)
    live_rows = three_index[picked].reshape(live_total * TB * TB, NAUX)
    block_width = 256
    block_total = NAUX // block_width

    def column_block(block_index):
        column_part = lax.dynamic_slice_in_dim(tile_grid, block_index * block_width, block_width, 4).astype(jnp.float32)
        half_virt = jnp.einsum('djksv,dkmvq->djmsq', virt_pairs, column_part).astype(jnp.bfloat16)
        sources_flat = half_virt.reshape(tile_total, TB, TB * block_width).astype(jnp.float32)
        summed = jnp.zeros((live_total, TB, TB * block_width), jnp.float32)
        for neighbour in range(3):
            summed = summed + jnp.einsum('tlm,tmx->tlx', occ_rows[:, neighbour], sources_flat[sources[:, neighbour]])
        full_virt = summed.astype(jnp.bfloat16).reshape(live_total * TB * TB, block_width)
        return jnp.dot(live_rows.T, full_virt, preferred_element_type=jnp.float32)
    columns = lax.map(column_block, jnp.arange(block_total, dtype=jnp.int32))
    polarizability = jnp.transpose(columns, (1, 0, 2)).reshape(NAUX, NAUX)
    return polarizability * (1.0 / math.sqrt(TB * TB * NBLK * TPD))
```

```python
import functools
import math

import jax
import jax.numpy as jnp
from jax import lax
from jax.experimental import pallas as pl
from jax.experimental.pallas import tpu as pltpu
from jax.sharding import PartitionSpec as P

NX, NY, NZ = 4, 4, 8
NG = 2 * NX
W = 4
TB = 32
HB = TB // 2
QL = 512
QH = QL // 2
LIVE = 128
RANKS = NG * NZ
MESH = pl.DeviceIdType.MESH
BF, F32 = jnp.bfloat16, jnp.float32


def tables(tile_shift, tile_count, block_owner):
    pairs = RANKS
    ids = jnp.arange(pairs, dtype=jnp.int32)
    row_block = jnp.sum(jnp.where(block_owner[None, :] == ids[:, None], ids[None, :], 0), axis=1)

    def by_plane(a):
        return a.reshape((NX, NZ, 2) + a.shape[1:]).swapaxes(0, 1).reshape((NZ, NG) + a.shape[1:])

    count = by_plane(tile_count)
    shift = by_plane(tile_shift)
    row = by_plane(row_block)
    before = (jnp.arange(NG)[None, :] < jnp.arange(NG)[:, None]).astype(jnp.int32)
    in_plane = jnp.sum(count[:, None, :] * before[None], axis=2)
    plane_total = jnp.sum(count, axis=1)
    before_z = (jnp.arange(NZ)[None, :] < jnp.arange(NZ)[:, None]).astype(jnp.int32)
    plane_start = jnp.sum(plane_total[None, :] * before_z, axis=1)
    slot = jnp.arange(W, dtype=jnp.int32)
    live = slot[None, None, :] < count[:, :, None]
    place = in_plane[:, :, None] + slot
    packed = jnp.arange(NZ, dtype=jnp.int32)[:, None, None] * 32 + place
    rank = plane_start[:, None, None] + place

    k = jnp.arange(32, dtype=jnp.int32)
    hit = (place[:, None] == k[None, :, None, None]) & live[:, None]
    g4 = jnp.arange(NG, dtype=jnp.int32)[:, None] * W
    list_t = jnp.sum(jnp.where(hit, (g4 + slot)[None, None], 0), axis=(2, 3))
    list_h = jnp.sum(jnp.where(hit, (g4 + shift)[:, None], 0), axis=(2, 3))
    first = jnp.where(k[None, :] < plane_total[:, None], 0, shift[:, 0, 0][:, None])
    list_h = list_h + first

    key = (row[:, :, None] * W + shift).reshape(-1)
    live_f = live.reshape(-1)
    packed_f = packed.reshape(-1)
    r = jnp.arange(LIVE, dtype=jnp.int32)
    by_rank = (rank.reshape(-1)[None, :] == r[:, None]) & live_f[None, :]
    rank_packed = jnp.sum(jnp.where(by_rank, packed_f[None], 0), axis=1)
    rank_key = jnp.sum(jnp.where(by_rank, key[None], 0), axis=1)
    mu = rank_key // W
    w = rank_key % W
    near = jnp.arange(3, dtype=jnp.int32) - 1
    near_w = w[:, None] - near
    near_key = (mu[:, None] + near) % RANKS * W + near_w
    match = (near_key[:, :, None] == key) & live_f & ((near_w >= 0) & (near_w < W))[:, :, None]
    found = jnp.sum(jnp.where(match, packed_f + 1, 0), axis=2)
    source = jnp.where(found > 0, found - 1, rank_packed[:, None])
    valid = (found > 0).astype(jnp.int32)

    def block_place(b):
        return (2 * (b // (2 * NZ)) + b % 2) * NZ + b // 2 % NZ

    return (
        row_block,
        list_t,
        list_h,
        rank_packed,
        block_place(mu),
        source.reshape(-1),
        valid.reshape(-1),
        block_place,
    )


def kernel(
    cap,
    list_t,
    list_h,
    rank_at,
    rank_row,
    rank_src,
    rank_ok,
    own_tab,
    tnat_h,
    tsm_h,
    comb_h,
    out,
    tnat,
    comb,
    hs,
    hbuf,
    txr0, txr1, txr2, txr3, txr4, txr5, txr6, txr7,
    hxr0, hxr1, hxr2, hxr3, hxr4, hxr5, hxr6, hxr7,
    tc,
    hc,
    tz,
    hz,
    at,
    fbuf,
    frecv,
    pbuf,
    prx,
    rxs,
    rxr,
    rzs,
    rzr,
    sems,
    txr_s,
    tzr_s,
    hxr_s,
    hzr_s,
    ys_s,
    yr_s,
    cs_s,
    cr_s,
    loc_s,
    own_s,
    out_s,
):
    txr = (txr0, txr1, txr2, txr3, txr4, txr5, txr6, txr7)
    hxr = (hxr0, hxr1, hxr2, hxr3, hxr4, hxr5, hxr6, hxr7)
    pi = lax.axis_index("pair")
    y = lax.axis_index("aux")
    c = pi % 2
    z = pi // 2 % NZ
    x = pi // (2 * NZ)
    g = 2 * x + c

    def dev_g(gg):
        return ((gg // 2 * NZ + z) * 2 + gg % 2, y)

    def dev_z(zz):
        return ((x * NZ + zz) * 2 + c, y)

    yp, ym = (y + 1) % NY, (y + NY - 1) % NY
    core = dev_g(g + 1 - 2 * c)

    def remote(src, dst, send, recv, device):
        return pltpu.make_async_remote_copy(
            src_ref=src, dst_ref=dst, send_sem=send, recv_sem=recv, device_id=device, device_id_type=MESH
        )

    def wait_bytes(ref, sem):
        pltpu.make_async_copy(ref, ref, sem).wait()

    barrier = pltpu.get_barrier_semaphore()
    for i in range(1, NG):
        pl.semaphore_signal(barrier, inc=1, device_id=dev_g((g + i) % NG), device_id_type=MESH)
    for i in range(1, NZ):
        pl.semaphore_signal(barrier, inc=1, device_id=dev_z((z + i) % NZ), device_id_type=MESH)
    pl.semaphore_signal(barrier, inc=1, device_id=(pi, yp), device_id_type=MESH)
    pl.semaphore_signal(barrier, inc=1, device_id=(pi, ym), device_id_type=MESH)

    own_t, own_h = [], []
    for k in range(NZ):
        zb = (z + 4 + k) % NZ
        own_t.append(
            pltpu.make_async_copy(
                tsm_h.at[x * NZ + zb, :, pl.ds(HB * c, HB), :], txr[k].at[pl.ds(W * g, W)], own_s.at[k]
            )
        )
        own_t[k].start()
    nat = pltpu.make_async_copy(tnat_h, tnat, loc_s.at[1])
    nat.start()
    own_c = pltpu.make_async_copy(comb_h, comb.at[g * NZ + z], loc_s.at[2])
    own_c.start()
    pl.semaphore_wait(barrier, NG + NZ)

    for i in range(1, NZ):
        remote(comb_h, comb.at[g * NZ + z], cs_s.at[0], cr_s.at[0], dev_z((z + i) % NZ)).start()

    for k in range(NZ):
        zb = (z + 4 + k) % NZ
        for i in range(1, NG):
            gg = (g + i) % NG
            remote(
                tsm_h.at[gg // 2 * NZ + zb, :, pl.ds(HB * (gg % 2), HB), :],
                txr[k].at[pl.ds(W * g, W)],
                out_s.at[k],
                txr_s.at[k],
                dev_g(gg),
            ).start()

    own_c.wait()
    wait_bytes(comb.at[pl.ds(0, NZ - 1)], cr_s.at[0])
    for i in range(1, NX):
        remote(
            comb.at[pl.ds(g * NZ, NZ)], comb.at[pl.ds(g * NZ, NZ)], cs_s.at[1], cr_s.at[1], dev_g((g + 2 * i) % NG)
        ).start()
    remote(comb.at[pl.ds(g * NZ, NZ)], comb.at[pl.ds(g * NZ, NZ)], cs_s.at[1], cr_s.at[1], core).start()
    wait_bytes(comb.at[pl.ds(0, NX * NZ)], cr_s.at[1])
    for i in range(1, NX):
        gg = (g + 2 * i) % NG
        remote(comb.at[pl.ds(gg * NZ, NZ)], comb.at[pl.ds(gg * NZ, NZ)], cs_s.at[2], cr_s.at[2], core).start()

    def t_step(k):
        zb = (z + 4 + k) % NZ
        own_t[k].wait()
        wait_bytes(txr[k].at[pl.ds(0, (NG - 1) * W)], txr_s.at[k])
        if k == 4:

            @pl.loop(0, cap)
            def _(i):
                tz[z, i] = txr[k][list_t[i]]

        else:

            @pl.loop(0, cap)
            def _(i):
                tc[zb, i] = txr[k][list_t[i]]

            remote(tc.at[zb], tz.at[z], sems.at[1], tzr_s.at[z], dev_z(zb)).start()

    for k in range(4):
        t_step(k)

    wait_bytes(comb.at[pl.ds(0, (NX - 1) * NZ)], cr_s.at[2])
    nat.wait()
    lane = lax.broadcasted_iota(jnp.int32, (TB, W * TB), 1) // TB
    keep = lane < 0
    for kk in range(W):
        keep = keep | ((lane == kk) & (own_tab[W + kk] > 0))
    rows = []
    for ww in range(W):
        band = comb[own_tab[ww], :, 0:256].astype(F32)
        band = pltpu.roll(band, (256 - TB * (W - 1 - ww)) % 256, 1)[:, : W * TB]
        rows.append(jnp.where(keep, band, 0.0).astype(BF))
    vmat = jnp.concatenate(rows, axis=0)
    slots = [own_tab[2 * W + ww] for ww in range(W)]

    for qh in range(2):

        @pl.loop(0, 2)
        def _(mh):
            @pl.loop(0, HB)
            def _(mi):
                rhs = jnp.concatenate(
                    [tnat[slots[ww], mh * HB + mi, :, qh * QH : (qh + 1) * QH] for ww in range(W)], axis=0
                )
                hs[mi] = jnp.dot(vmat, rhs, preferred_element_type=F32)

            for ww in range(W):

                @pl.loop(0, TB // 8)
                def _(sb):
                    part = hs[:, pl.ds(ww * TB + sb * 8, 8), :]
                    hbuf[qh, pl.ds(sb * 8, 8), ww, pl.ds(mh * HB, HB), :] = jnp.swapaxes(part, 0, 1).astype(BF)

    for k in range(NZ):
        zb = (z + 4 + k) % NZ
        own_h.append(pltpu.make_async_copy(hbuf.at[c, x * NZ + zb], hxr[k].at[pl.ds(W * g, W)], own_s.at[NZ + k]))
        own_h[k].start()
        for i in range(1, NG):
            gg = (g + i) % NG
            remote(
                hbuf.at[gg % 2, gg // 2 * NZ + zb], hxr[k].at[pl.ds(W * g, W)], out_s.at[NZ + k], hxr_s.at[k], dev_g(gg)
            ).start()

    for k in range(4, NZ):
        t_step(k)

    def h_step(k):
        zb = (z + 4 + k) % NZ
        own_h[k].wait()
        wait_bytes(hxr[k].at[pl.ds(0, (NG - 1) * W)], hxr_s.at[k])
        if k == 4:

            @pl.loop(0, cap)
            def _(i):
                hz[z, i] = hxr[k][list_h[i]]

        else:

            @pl.loop(0, cap)
            def _(i):
                hc[zb, i] = hxr[k][list_h[i]]

            remote(hc.at[zb], hz.at[z], sems.at[3], hzr_s.at[z], dev_z(zb)).start()

    h_step(0)
    h_step(1)

    for i in range(1, NZ):
        zz = (z + i) % NZ
        wait_bytes(tz.at[zz], tzr_s.at[zz])

    @pl.loop(0, LIVE // 8)
    def _(b):
        tiles = []
        for i in range(8):
            p = rank_at[b * 8 + i]
            tiles.append(tz[p // 32, p % 32])
        at[y, :, pl.ds(b * 128, 128)] = jnp.concatenate(tiles, axis=0).T

    lo, hi = pl.ds(0, QH), pl.ds(QH, QH)
    remote(at.at[y, lo], at.at[y, lo], ys_s.at[0], yr_s.at[0], (pi, yp)).start()
    remote(at.at[y, hi], at.at[y, hi], ys_s.at[1], yr_s.at[1], (pi, ym)).start()
    remote(at.at[y, hi], at.at[y, hi], ys_s.at[2], yr_s.at[2], (pi, yp)).start()
    remote(at.at[y, lo], at.at[y, lo], ys_s.at[3], yr_s.at[3], (pi, ym)).start()

    for k in range(2, 6):
        h_step(k)
    wait_bytes(at.at[ym, lo], yr_s.at[0])
    remote(at.at[ym, lo], at.at[ym, lo], ys_s.at[4], yr_s.at[4], (pi, yp)).start()
    wait_bytes(at.at[yp, hi], yr_s.at[1])
    remote(at.at[yp, hi], at.at[yp, hi], ys_s.at[5], yr_s.at[5], (pi, ym)).start()
    for k in range(6, NZ):
        h_step(k)

    for i in range(1, NZ):
        zz = (z + i) % NZ
        wait_bytes(hz.at[zz], hzr_s.at[zz])
    lane3 = lax.broadcasted_iota(jnp.int32, (TB, 3 * TB), 1) // TB

    @pl.loop(0, LIVE)
    def _(t):
        occ = comb[rank_row[t], :, 256 : 256 + 3 * TB]
        src, use = [], lane3 < 0
        for r in range(3):
            p = rank_src[3 * t + r]
            src.append(hz[p // 32, p % 32])
            use = use | ((lane3 == r) & (rank_ok[3 * t + r] > 0))
        occ = jnp.where(use, occ.astype(F32), 0.0).astype(BF)
        f = jnp.dot(occ, jnp.concatenate(src, axis=0), preferred_element_type=F32).astype(BF)
        fbuf[0, t] = f[:HB]
        fbuf[1, t] = f[HB:]

    swap = remote(fbuf.at[1 - c], frecv, sems.at[4], sems.at[5], core)
    swap.start()
    for i, ref in ((2, at.at[ym, hi]), (3, at.at[yp, lo]), (4, at.at[(y + 2) % NY, lo]), (5, at.at[(y + 2) % NY, hi])):
        wait_bytes(ref, yr_s.at[i])
    swap.wait_recv()

    own_q = pl.ds(pl.multiple_of(c * QH, QH), QH)
    far_q = pl.ds(pl.multiple_of((1 - c) * QH, QH), QH)

    def core_sum(i):
        xb = (x + 1 + i) % NX
        wait_bytes(prx.at[i], sems.at[8 + i])
        return pbuf[xb, :, c] + prx[i]

    def ship(i):
        xb = (x + 1 + i) % NX
        rxs[i] = core_sum(i).astype(BF)
        remote(rxs.at[i], rxr.at[i], sems.at[12 + i], sems.at[15 + i], dev_g(2 * xb + c)).start()

    for i in range(NX):
        xb = (x + 1 + i) % NX

        @pl.loop(0, 4)
        def _(mt):
            lhs = at[xb, pl.ds(mt * 128, 128), :]
            own = jnp.dot(lhs, fbuf[c].reshape(LIVE * HB, QH), preferred_element_type=F32)
            far = jnp.dot(lhs, frecv[...].reshape(LIVE * HB, QH), preferred_element_type=F32)
            pbuf[xb, pl.ds(mt * 2, 2), :, :, own_q] = own.reshape(2, 2, TB, QH)
            pbuf[xb, pl.ds(mt * 2, 2), :, :, far_q] = far.reshape(2, 2, TB, QH)

        remote(pbuf.at[xb, :, 1 - c], prx.at[i], sems.at[18 + i], sems.at[8 + i], core).start()
        if i > 0:
            ship(i - 1)

    total = core_sum(NX - 1)
    for i in range(NX - 1):
        wait_bytes(rxr.at[i], sems.at[15 + i])
        total = total + rxr[i].astype(F32)
    rzs[...] = total.astype(BF)
    for i in range(1, NZ):
        zz = (z + i) % NZ
        remote(rzs.at[zz], rzr.at[z], sems.at[6], sems.at[7], dev_z(zz)).start()
    rzr[z] = rzs[z]
    wait_bytes(rzs.at[pl.ds(0, NZ - 1)], sems.at[7])
    final = rzr[0].astype(F32)
    for zz in range(1, NZ):
        final = final + rzr[zz].astype(F32)
    out[...] = final * (1.0 / math.sqrt(TB * TB * LIVE))

    wait_bytes(comb.at[pl.ds(0, NZ - 1)], cs_s.at[0])
    wait_bytes(comb.at[pl.ds(0, NX * NZ)], cs_s.at[1])
    wait_bytes(comb.at[pl.ds(0, (NX - 1) * NZ)], cs_s.at[2])
    for k in range(NZ):
        wait_bytes(txr[k].at[pl.ds(0, (NG - 1) * W)], out_s.at[k])
    wait_bytes(tc.at[pl.ds(0, NZ - 1)], sems.at[1])
    for k in range(NZ):
        wait_bytes(hxr[k].at[pl.ds(0, (NG - 1) * W)], out_s.at[NZ + k])
    wait_bytes(hc.at[pl.ds(0, NZ - 1)], sems.at[3])
    swap.wait_send()
    wait_bytes(rzs.at[pl.ds(0, NZ - 1)], sems.at[6])
    for i in range(6):
        wait_bytes(at.at[y, lo], ys_s.at[i])
    for i in range(NX - 1):
        wait_bytes(rxs.at[i], sems.at[12 + i])
    for i in range(NX):
        wait_bytes(prx.at[i], sems.at[18 + i])


def fused(cap, cid, tabs, tnat, tsm, comb):
    smem = pl.BlockSpec(memory_space=pltpu.SMEM)
    hbm = pl.BlockSpec(memory_space=pl.ANY)
    dma = pltpu.SemaphoreType.DMA
    return pl.pallas_call(
        functools.partial(kernel, cap),
        out_shape=jax.ShapeDtypeStruct((TB, QL), F32),
        in_specs=[smem] * 7 + [hbm] * 3,
        out_specs=pl.BlockSpec(memory_space=pltpu.VMEM),
        scratch_shapes=[
            pltpu.VMEM((W, TB, TB, QL), BF),
            pltpu.VMEM((RANKS, TB, 384), BF),
            pltpu.VMEM((HB, W * TB, QH), F32),
            pltpu.VMEM((2, TB, W, TB, QH), BF),
        ]
        + [pltpu.VMEM((NG * W, HB, QL), BF)] * NZ
        + [pltpu.VMEM((NG * W, TB, QH), BF)] * NZ
        + [
            pltpu.VMEM((NZ, cap, HB, QL), BF),
            pltpu.VMEM((NZ, cap, TB, QH), BF),
            pltpu.VMEM((NZ, cap, HB, QL), BF),
            pltpu.VMEM((NZ, cap, TB, QH), BF),
            pltpu.VMEM((NY, QL, LIVE * HB), BF),
            pltpu.VMEM((2, LIVE, HB, QH), BF),
            pltpu.VMEM((LIVE, HB, QH), BF),
            pltpu.VMEM((NX, NZ, 2, TB, QL), F32),
            pltpu.VMEM((NX, NZ, TB, QL), F32),
            pltpu.VMEM((NX - 1, NZ, TB, QL), BF),
            pltpu.VMEM((NX - 1, NZ, TB, QL), BF),
            pltpu.VMEM((NZ, TB, QL), BF),
            pltpu.VMEM((NZ, TB, QL), BF),
            dma((22,)),
            dma((NZ,)),
            dma((NZ,)),
            dma((NZ,)),
            dma((NZ,)),
            dma((6,)),
            dma((6,)),
            dma((3,)),
            dma((3,)),
            dma((4,)),
            dma((2 * NZ,)),
            dma((2 * NZ,)),
        ],
        compiler_params=pltpu.CompilerParams(
            collective_id=cid, has_side_effects=True, vmem_limit_bytes=62 * 2**20
        ),
    )(*tabs, tnat, tsm, comb)


def per_device(three_index, occ_blocks, virt_blocks, tile_shift, tile_count, block_owner):
    pos = lax.axis_index("pair")
    z = pos // 2 % NZ
    row_block, list_t, list_h, rank_at, rank_row, rank_src, rank_ok, block_place = tables(
        tile_shift, tile_count, block_owner
    )
    own_shift = lax.dynamic_index_in_dim(tile_shift, pos, 0, keepdims=False)
    own_count = lax.dynamic_index_in_dim(tile_count, pos, 0, keepdims=False)
    own_row = lax.dynamic_index_in_dim(row_block, pos, 0, keepdims=False)
    window = jnp.arange(W, dtype=jnp.int32)
    slot_of = jnp.sum(jnp.where(own_shift[None, :] == window[:, None], window[None, :], 0), axis=1)
    own_tab = jnp.concatenate(
        [block_place((own_row + window - 2) % RANKS), (slot_of < own_count).astype(jnp.int32), slot_of]
    )
    tabs = (
        lax.dynamic_index_in_dim(list_t, z, 0, keepdims=False),
        lax.dynamic_index_in_dim(list_h, z, 0, keepdims=False),
        rank_at,
        rank_row,
        rank_src,
        rank_ok,
        own_tab,
    )
    tsm = jnp.transpose(three_index, (2, 0, 1, 3))
    virt = jnp.transpose(virt_blocks[0], (1, 0, 2)).reshape(TB, 7 * TB)
    occ = jnp.transpose(occ_blocks[0], (1, 0, 2)).reshape(TB, 3 * TB)
    comb = jnp.concatenate([virt, jnp.zeros((TB, TB), BF), occ, jnp.zeros((TB, TB), BF)], axis=1)
    plane = jnp.max(jnp.sum(tile_count.reshape(NX, NZ, 2), axis=(0, 2)))
    return lax.cond(
        plane <= 20,
        functools.partial(fused, 20, 1),
        functools.partial(fused, 32, 2),
        tabs,
        three_index,
        tsm,
        comb,
    )


def solution(mesh):
    in_specs = (
        P("pair", None, None, "aux"),
        P("pair", None, None, None),
        P("pair", None, None, None),
        P(),
        P(),
        P(),
    )
    return jax.shard_map(per_device, mesh=mesh, in_specs=in_specs, out_specs=P("pair", "aux"), check_vma=False)
```

```python
import functools
import math

import jax
import jax.numpy as jnp
from jax import lax
from jax.experimental import pallas as pl
from jax.experimental.pallas import tpu as pltpu
from jax.sharding import PartitionSpec as P

NX, NY, NZ = 4, 4, 8
NG = 2 * NX
W = 4
TB = 32
HB = TB // 2
QL = 512
QH = QL // 2
LIVE = 128
RANKS = NG * NZ
OFF = (4, 3, 5, 2, 6, 1, 7, 0)
AHEAD = 2
CAPS = (20, 22, 24, 32)
MESH = pl.DeviceIdType.MESH
BF, F32 = jnp.bfloat16, jnp.float32


def fill_tables(pi, z, count, owner, shift, tab):
    tiles = RANKS * W

    def grid(lanes):
        return lax.broadcasted_iota(jnp.int32, (tiles, lanes), 0), lax.broadcasted_iota(jnp.int32, (tiles, lanes), 1)

    def pick(cond, value):
        return jnp.sum(jnp.where(cond, value, 0), axis=1, keepdims=True)

    def gather(cond, value):
        return jnp.sum(jnp.where(cond, value, 0), axis=0, keepdims=True)

    t, d = grid(RANKS)
    td = t // W
    zt, zd = td // 2 % NZ, d // 2 % NZ
    count_t = pick(d == td, count)
    before = pick((zd == zt) & (d < td), count)
    start = pick(zd < zt, count)
    row = pick(owner == td, d)
    tt, lane = grid(tiles)
    sub = lax.broadcasted_iota(jnp.int32, (RANKS, tiles), 0)
    at_lane = lax.broadcasted_iota(jnp.int32, (RANKS, tiles), 1)
    shift_r = jnp.zeros((1, tiles), jnp.int32)
    for jj in range(W):
        shift_r = shift_r + gather((at_lane // W == sub) & (at_lane % W == jj), shift[:, jj : jj + 1])
    shift_t = pick(tt == lane, shift_r)

    t, r = grid(128)
    j, td = t % W, t // W
    zt = td // 2 % NZ
    gt = 2 * (td // (2 * NZ)) + td % 2
    live = j < count_t
    place = before + j
    packed = zt * 32 + place
    key = row * W + shift_t
    by_rank = (start + place == r) & live
    rank_packed = gather(by_rank, packed)
    rank_key = gather(by_rank, key)
    mu, w = rank_key // W, rank_key % W

    def block_place(b):
        return (2 * (b // (2 * NZ)) + b % 2) * NZ + b // 2 % NZ

    tab[0:1, :] = rank_packed
    tab[1:2, :] = block_place(mu)
    for n in range(3):
        near_w = w + 1 - n
        near_key = ((mu + RANKS + n - 1) % RANKS) * W + near_w
        match = (key == near_key) & live & (near_w >= 0) & (near_w < W)
        found = gather(match, packed + 1)
        tab[2 + n : 3 + n, :] = jnp.where(found > 0, found - 1, rank_packed)
        tab[5 + n : 6 + n, :] = jnp.where(found > 0, 1, 0)
    in_plane = (zt == z) & live
    hit = in_plane & (place == r)
    tab[8:9, :] = gather(hit, gt * W + j)
    spare = r[0:1, :] >= gather(in_plane, 1)
    first = gather(in_plane & (place == 0), shift_t)
    tab[9:10, :] = gather(hit, gt * W + shift_t) + jnp.where(spare, first, 0)
    own = td == pi
    own_row = gather(own & (j == 0), row)
    tab[10:11, :] = block_place((own_row + RANKS + r[0:1, :] - 2) % RANKS)
    tab[11:12, :] = gather(own & live & (shift_t == r), 1)
    tab[12:13, :] = jnp.minimum(gather(own & (shift_t == r), j), W - 1)
    tab[13:16, :] = jnp.zeros((3, 128), jnp.int32)


def kernel(
    cap,
    count_v,
    owner_v,
    shift_v,
    virt_v,
    occ_v,
    tnat_h,
    out,
    tab_v,
    tab,
    tnat,
    ts,
    comb,
    hs,
    hbuf,
    txr0, txr1, txr2, txr3, txr4, txr5, txr6, txr7,
    hxr0, hxr1, hxr2, hxr3, hxr4, hxr5, hxr6, hxr7,
    tc,
    hc,
    tz,
    hz,
    at,
    fbuf,
    fout,
    pbuf,
    prx,
    rxs,
    rxr,
    rzs,
    rzr,
    sems,
    txr_s,
    tzr_s,
    hxr_s,
    hzr_s,
    ys_s,
    yr_s,
    cs_s,
    cr_s,
    loc_s,
    own_s,
    out_s,
    ps_s,
    pr_s,
    xs_s,
    xr_s,
):
    txr = (txr0, txr1, txr2, txr3, txr4, txr5, txr6, txr7)
    hxr = (hxr0, hxr1, hxr2, hxr3, hxr4, hxr5, hxr6, hxr7)
    pi = lax.axis_index("pair")
    y = lax.axis_index("aux")
    c = pi % 2
    z = pi // 2 % NZ
    x = pi // (2 * NZ)
    g = 2 * x + c

    def dev_g(gg):
        return ((gg // 2 * NZ + z) * 2 + gg % 2, y)

    def dev_z(zz):
        return ((x * NZ + zz) * 2 + c, y)

    yp, ym = (y + 1) % NY, (y + NY - 1) % NY
    core = dev_g(g + 1 - 2 * c)

    def remote(src, dst, send, recv, device):
        return pltpu.make_async_remote_copy(
            src_ref=src, dst_ref=dst, send_sem=send, recv_sem=recv, device_id=device, device_id_type=MESH
        )

    def wait_bytes(ref, sem):
        pltpu.make_async_copy(ref, ref, sem).wait()

    barrier = pltpu.get_barrier_semaphore()
    for i in range(1, NG):
        pl.semaphore_signal(barrier, inc=1, device_id=dev_g((g + i) % NG), device_id_type=MESH)
    for i in range(1, NZ):
        pl.semaphore_signal(barrier, inc=1, device_id=dev_z((z + i) % NZ), device_id_type=MESH)
    pl.semaphore_signal(barrier, inc=1, device_id=(pi, yp), device_id_type=MESH)
    pl.semaphore_signal(barrier, inc=1, device_id=(pi, ym), device_id_type=MESH)

    own_t, own_h = [], []
    nat = pltpu.make_async_copy(tnat_h, tnat, loc_s.at[1])
    nat.start()
    gap = jnp.zeros((TB, TB), BF)
    blocks = [virt_v[0, i] for i in range(7)] + [gap] + [occ_v[0, i] for i in range(3)] + [gap]
    comb[g * NZ + z] = jnp.concatenate(blocks, axis=1)
    nat.wait()

    def split(st):
        @pl.loop(0, W)
        def _(j):
            for mh in range(2):
                for q in range(0, QL, 128):
                    part = tnat[j, mh * HB : (mh + 1) * HB, pl.ds(pl.multiple_of(st * HB, HB), HB), q : q + 128]
                    part = jnp.swapaxes(part.astype(F32), 0, 1).astype(BF)
                    ts[pl.ds(st * HB, HB), j, mh * HB : (mh + 1) * HB, q : q + 128] = part

    first = (z + OFF[0]) % NZ // (NZ // 2)
    split(first)
    pl.semaphore_wait(barrier, NG + NZ)

    for i in range(1, NZ):
        remote(comb.at[g * NZ + z], comb.at[g * NZ + z], cs_s.at[0], cr_s.at[0], dev_z((z + i) % NZ)).start()

    def t_send(k):
        zb = (z + OFF[k]) % NZ
        own_t.append(
            pltpu.make_async_copy(
                ts.at[zb * NX + x, :, pl.ds(HB * c, HB), :], txr[k].at[pl.ds(W * g, W)], own_s.at[k]
            )
        )
        own_t[k].start()
        for i in range(1, NG):
            gg = (g + i) % NG
            remote(
                ts.at[zb * NX + gg // 2, :, pl.ds(HB * (gg % 2), HB), :],
                txr[k].at[pl.ds(W * g, W)],
                out_s.at[k],
                txr_s.at[k],
                dev_g(gg),
            ).start()

    t_send(0)
    split(1 - first)
    for k in range(1, AHEAD):
        t_send(k)

    fill_tables(pi, z, count_v[...], owner_v[...], shift_v[...], tab_v)
    tab_c = pltpu.make_async_copy(tab_v, tab, loc_s.at[0])
    tab_c.start()
    tab_c.wait()

    def t_step(k):
        zb = (z + OFF[k]) % NZ
        own_t[k].wait()
        wait_bytes(txr[k].at[pl.ds(0, (NG - 1) * W)], txr_s.at[k])
        if k + AHEAD < NZ:
            t_send(k + AHEAD)
        if OFF[k] == 0:

            @pl.loop(0, cap)
            def _(i):
                tz[z, i] = txr[k][tab[8, i]]

        else:

            @pl.loop(0, cap)
            def _(i):
                tc[zb, i] = txr[k][tab[8, i]]

            remote(tc.at[zb], tz.at[z], sems.at[1], tzr_s.at[z], dev_z(zb)).start()

    t_step(0)
    wait_bytes(comb.at[pl.ds(0, NZ - 1)], cr_s.at[0])
    for i in range(1, NX):
        remote(
            comb.at[pl.ds(g * NZ, NZ)], comb.at[pl.ds(g * NZ, NZ)], cs_s.at[1], cr_s.at[1], dev_g((g + 2 * i) % NG)
        ).start()
    remote(comb.at[pl.ds(g * NZ, NZ)], comb.at[pl.ds(g * NZ, NZ)], cs_s.at[1], cr_s.at[1], core).start()
    t_step(1)
    wait_bytes(comb.at[pl.ds(0, NX * NZ)], cr_s.at[1])
    for i in range(1, NX):
        gg = (g + 2 * i) % NG
        remote(comb.at[pl.ds(gg * NZ, NZ)], comb.at[pl.ds(gg * NZ, NZ)], cs_s.at[2], cr_s.at[2], core).start()
    t_step(2)

    wait_bytes(comb.at[pl.ds(0, (NX - 1) * NZ)], cr_s.at[2])
    lane = lax.broadcasted_iota(jnp.int32, (TB, W * TB), 1) // TB
    keep = lane < 0
    for kk in range(W):
        keep = keep | ((lane == kk) & (tab[11, kk] > 0))
    rows = []
    for ww in range(W):
        band = comb[tab[10, ww], :, 0:256].astype(F32)
        band = pltpu.roll(band, (256 - TB * (W - 1 - ww)) % 256, 1)[:, : W * TB]
        rows.append(jnp.where(keep, band, 0.0).astype(BF))
    vmat = jnp.concatenate(rows, axis=0)
    slots = [tab[12, ww] for ww in range(W)]

    def h_form(qh, mh):
        @pl.loop(0, HB)
        def _(mi):
            rhs = jnp.concatenate(
                [tnat[slots[ww], mh * HB + mi, :, qh * QH : (qh + 1) * QH] for ww in range(W)], axis=0
            )
            hs[mi] = jnp.dot(vmat, rhs, preferred_element_type=F32)

        for ww in range(W):

            @pl.loop(0, TB // 8)
            def _(sb):
                part = hs[:, pl.ds(ww * TB + sb * 8, 8), :]
                hbuf[qh, pl.ds(sb * 8, 8), ww, mh * HB : (mh + 1) * HB, :] = jnp.swapaxes(part, 0, 1).astype(BF)

    for i in range(4):
        h_form(i // 2, i % 2)
        t_step(3 + i)

    def h_send(k):
        zb = (z + OFF[k]) % NZ
        own_h.append(pltpu.make_async_copy(hbuf.at[c, zb * NX + x], hxr[k].at[pl.ds(W * g, W)], own_s.at[NZ + k]))
        own_h[k].start()
        for i in range(1, NG):
            gg = (g + i) % NG
            remote(
                hbuf.at[gg % 2, zb * NX + gg // 2], hxr[k].at[pl.ds(W * g, W)], out_s.at[NZ + k], hxr_s.at[k], dev_g(gg)
            ).start()

    h_send(0)
    t_step(7)
    for k in range(1, AHEAD):
        h_send(k)

    def h_step(k):
        zb = (z + OFF[k]) % NZ
        own_h[k].wait()
        wait_bytes(hxr[k].at[pl.ds(0, (NG - 1) * W)], hxr_s.at[k])
        if k + AHEAD < NZ:
            h_send(k + AHEAD)
        if OFF[k] == 0:

            @pl.loop(0, cap)
            def _(i):
                hz[z, i] = hxr[k][tab[9, i]]

        else:

            @pl.loop(0, cap)
            def _(i):
                hc[zb, i] = hxr[k][tab[9, i]]

            remote(hc.at[zb], hz.at[z], sems.at[3], hzr_s.at[z], dev_z(zb)).start()

    h_step(0)
    h_step(1)

    for i in range(1, NZ):
        zz = (z + i) % NZ
        wait_bytes(tz.at[zz], tzr_s.at[zz])

    @pl.loop(0, LIVE // 8)
    def _(b):
        tiles = []
        for i in range(8):
            p = tab[0, b * 8 + i]
            tiles.append(tz[p // 32, p % 32])
        at[y, :, pl.ds(b * 128, 128)] = jnp.concatenate(tiles, axis=0).T

    lo, hi = pl.ds(0, QH), pl.ds(QH, QH)
    remote(at.at[y, lo], at.at[y, lo], ys_s.at[0], yr_s.at[0], (pi, yp)).start()
    remote(at.at[y, hi], at.at[y, hi], ys_s.at[1], yr_s.at[1], (pi, ym)).start()
    remote(at.at[y, hi], at.at[y, hi], ys_s.at[2], yr_s.at[2], (pi, yp)).start()
    remote(at.at[y, lo], at.at[y, lo], ys_s.at[3], yr_s.at[3], (pi, ym)).start()

    for k in range(2, 6):
        h_step(k)
    wait_bytes(at.at[ym, lo], yr_s.at[0])
    remote(at.at[ym, lo], at.at[ym, lo], ys_s.at[4], yr_s.at[4], (pi, yp)).start()
    wait_bytes(at.at[yp, hi], yr_s.at[1])
    remote(at.at[yp, hi], at.at[yp, hi], ys_s.at[5], yr_s.at[5], (pi, ym)).start()
    for k in range(6, NZ):
        h_step(k)

    for i in range(1, NZ):
        zz = (z + i) % NZ
        wait_bytes(hz.at[zz], hzr_s.at[zz])
    lane3 = lax.broadcasted_iota(jnp.int32, (TB, 3 * TB), 1) // TB

    @pl.loop(0, LIVE)
    def _(t):
        occ = comb[tab[1, t], :, 256 : 256 + 3 * TB]
        src, use = [], lane3 < 0
        for r in range(3):
            p = tab[2 + r, t]
            src.append(hz[p // 32, p % 32])
            use = use | ((lane3 == r) & (tab[5 + r, t] > 0))
        occ = jnp.where(use, occ.astype(F32), 0.0).astype(BF)
        f = jnp.dot(occ, jnp.concatenate(src, axis=0), preferred_element_type=F32).astype(BF)
        lower = c == 0
        fbuf[c, t] = jnp.where(lower, f[:HB], f[HB:])
        fout[t] = jnp.where(lower, f[HB:], f[:HB])

    swap = remote(fout, fbuf.at[c], sems.at[4], sems.at[5], core)
    swap.start()
    for i, ref in ((2, at.at[ym, hi]), (3, at.at[yp, lo]), (4, at.at[(y + 2) % NY, lo]), (5, at.at[(y + 2) % NY, hi])):
        wait_bytes(ref, yr_s.at[i])
    swap.wait_recv()

    def core_sum(h, i):
        xb = (x + 1 + i) % NX
        wait_bytes(prx.at[h, i], pr_s.at[NX * h + i])
        return pbuf[h, xb, :, c] + prx[h, i]

    def ship(h, i):
        xb = (x + 1 + i) % NX
        rxs[h, i] = core_sum(h, i).astype(BF)
        remote(rxs.at[h, i], rxr.at[h, i], xs_s.at[NX * h + i], xr_s.at[NX * h + i], dev_g(2 * xb + c)).start()

    for h in range(2):
        for i in range(NX):
            xb = (x + 1 + i) % NX

            @pl.loop(0, 4)
            def _(mt):
                term = jnp.dot(
                    at[xb, pl.ds(mt * 128, 128), :],
                    fbuf[h].reshape(LIVE * HB, QH),
                    preferred_element_type=F32,
                )
                pbuf[h, xb, pl.ds(mt * 2, 2)] = term.reshape(2, 2, TB, QH)

            remote(pbuf.at[h, xb, :, 1 - c], prx.at[h, i], ps_s.at[NX * h + i], pr_s.at[NX * h + i], core).start()
            if i > 0:
                ship(h, i - 1)

    for h in range(2):
        total = core_sum(h, NX - 1)
        for i in range(NX - 1):
            wait_bytes(rxr.at[h, i], xr_s.at[NX * h + i])
            total = total + rxr[h, i].astype(F32)
        rzs[h] = total.astype(BF)
        for i in range(1, NZ):
            zz = (z + i) % NZ
            remote(rzs.at[h, zz], rzr.at[h, z], sems.at[6 + h], sems.at[8 + h], dev_z(zz)).start()
        rzr[h, z] = rzs[h, z]
    for h in range(2):
        wait_bytes(rzs.at[h, pl.ds(0, NZ - 1)], sems.at[8 + h])
        final = rzr[h, 0].astype(F32)
        for zz in range(1, NZ):
            final = final + rzr[h, zz].astype(F32)
        out[:, h * QH : (h + 1) * QH] = final * (1.0 / math.sqrt(TB * TB * LIVE))

    wait_bytes(comb.at[pl.ds(0, NZ - 1)], cs_s.at[0])
    wait_bytes(comb.at[pl.ds(0, NX * NZ)], cs_s.at[1])
    wait_bytes(comb.at[pl.ds(0, (NX - 1) * NZ)], cs_s.at[2])
    for k in range(NZ):
        wait_bytes(txr[k].at[pl.ds(0, (NG - 1) * W)], out_s.at[k])
    wait_bytes(tc.at[pl.ds(0, NZ - 1)], sems.at[1])
    for k in range(NZ):
        wait_bytes(hxr[k].at[pl.ds(0, (NG - 1) * W)], out_s.at[NZ + k])
    wait_bytes(hc.at[pl.ds(0, NZ - 1)], sems.at[3])
    swap.wait_send()
    for i in range(6):
        wait_bytes(at.at[y, lo], ys_s.at[i])
    for h in range(2):
        wait_bytes(rzs.at[h, pl.ds(0, NZ - 1)], sems.at[6 + h])
        for i in range(NX - 1):
            wait_bytes(rxs.at[h, i], xs_s.at[NX * h + i])
        for i in range(NX):
            wait_bytes(prx.at[h, i], ps_s.at[NX * h + i])


def fused(cap, cid, *operands):
    vmem = pl.BlockSpec(memory_space=pltpu.VMEM)
    hbm = pl.BlockSpec(memory_space=pl.ANY)
    dma = pltpu.SemaphoreType.DMA
    return pl.pallas_call(
        functools.partial(kernel, cap),
        out_shape=jax.ShapeDtypeStruct((TB, QL), F32),
        in_specs=[vmem] * 5 + [hbm],
        out_specs=vmem,
        scratch_shapes=[
            pltpu.VMEM((16, 128), jnp.int32),
            pltpu.SMEM((16, 128), jnp.int32),
            pltpu.VMEM((W, TB, TB, QL), BF),
            pltpu.VMEM((TB, W, TB, QL), BF),
            pltpu.VMEM((RANKS, TB, 384), BF),
            pltpu.VMEM((HB, W * TB, QH), F32),
            pltpu.VMEM((2, TB, W, TB, QH), BF),
        ]
        + [pltpu.VMEM((NG * W, HB, QL), BF)] * NZ
        + [pltpu.VMEM((NG * W, TB, QH), BF)] * NZ
        + [
            pltpu.VMEM((NZ, cap, HB, QL), BF),
            pltpu.VMEM((NZ, cap, TB, QH), BF),
            pltpu.VMEM((NZ, cap, HB, QL), BF),
            pltpu.VMEM((NZ, cap, TB, QH), BF),
            pltpu.VMEM((NY, QL, LIVE * HB), BF),
            pltpu.VMEM((2, LIVE, HB, QH), BF),
            pltpu.VMEM((LIVE, HB, QH), BF),
            pltpu.VMEM((2, NX, NZ, 2, TB, QH), F32),
            pltpu.VMEM((2, NX, NZ, TB, QH), F32),
            pltpu.VMEM((2, NX - 1, NZ, TB, QH), BF),
            pltpu.VMEM((2, NX - 1, NZ, TB, QH), BF),
            pltpu.VMEM((2, NZ, TB, QH), BF),
            pltpu.VMEM((2, NZ, TB, QH), BF),
            dma((10,)),
            dma((NZ,)),
            dma((NZ,)),
            dma((NZ,)),
            dma((NZ,)),
            dma((6,)),
            dma((6,)),
            dma((3,)),
            dma((3,)),
            dma((4,)),
            dma((2 * NZ,)),
            dma((2 * NZ,)),
            dma((2 * NX,)),
            dma((2 * NX,)),
            dma((2 * NX,)),
            dma((2 * NX,)),
        ],
        compiler_params=pltpu.CompilerParams(
            collective_id=cid, has_side_effects=True, vmem_limit_bytes=62 * 2**20
        ),
    )(*operands)


def per_device(three_index, occ_blocks, virt_blocks, tile_shift, tile_count, block_owner):
    plane = jnp.max(jnp.sum(tile_count.reshape(NX, NZ, 2), axis=(0, 2)))
    need = jnp.sum(jnp.stack([plane > cap for cap in CAPS[:-1]]).astype(jnp.int32))
    return lax.switch(
        need,
        [functools.partial(fused, cap, 1 + i) for i, cap in enumerate(CAPS)],
        tile_count.reshape(1, RANKS),
        block_owner.reshape(1, RANKS),
        tile_shift,
        virt_blocks,
        occ_blocks,
        three_index,
    )


def solution(mesh):
    in_specs = (
        P("pair", None, None, "aux"),
        P("pair", None, None, None),
        P("pair", None, None, None),
        P(),
        P(),
        P(),
    )
    return jax.shard_map(per_device, mesh=mesh, in_specs=in_specs, out_specs=P("pair", "aux"), check_vma=False)
```

```python
import functools
import math

import jax
import jax.numpy as jnp
import numpy as np
from jax import lax
from jax.experimental import pallas as pl
from jax.experimental.pallas import tpu as pltpu
from jax.sharding import PartitionSpec as P

NX, NY, NZ = 4, 4, 8
NG = 2 * NX
W = 4
TB = 32
HB = TB // 2
QL = 512
QH = QL // 2
LIVE = 128
RANKS = NG * NZ
OFF = (4, 3, 5, 2, 6, 1, 7, 0)
NA = 5
AHEAD = 2
SIZES = ((19, 64), (20, 64), (21, 64), (23, 64), (32, 32))
MESH = pl.DeviceIdType.MESH
BF, F32 = jnp.bfloat16, jnp.float32


def fill_tables(pi, z, count, owner, shift, tab):
    tiles = RANKS * W

    def grid(lanes):
        return lax.broadcasted_iota(jnp.int32, (tiles, lanes), 0), lax.broadcasted_iota(jnp.int32, (tiles, lanes), 1)

    def pick(cond, value):
        return jnp.sum(jnp.where(cond, value, 0), axis=1, keepdims=True)

    def gather(cond, value):
        return jnp.sum(jnp.where(cond, value, 0), axis=0, keepdims=True)

    t, d = grid(RANKS)
    td = t // W
    zt, zd = td // 2 % NZ, d // 2 % NZ

    def step_of(plane):
        away = (z + NZ - plane) % NZ
        return sum(jnp.where(away == OFF[k], k, 0) for k in range(NZ))

    step_t = step_of(zt)
    count_t = pick(d == td, count)
    before = pick((zd == zt) & (d < td), count)
    start = pick(step_of(zd) < step_t, count)
    row = pick(owner == td, d)
    step_t = step_t[:, 0:1]
    tt, lane = grid(tiles)
    sub = lax.broadcasted_iota(jnp.int32, (RANKS, tiles), 0)
    at_lane = lax.broadcasted_iota(jnp.int32, (RANKS, tiles), 1)
    shift_r = jnp.zeros((1, tiles), jnp.int32)
    for jj in range(W):
        shift_r = shift_r + gather((at_lane // W == sub) & (at_lane % W == jj), shift[:, jj : jj + 1])
    shift_t = pick(tt == lane, shift_r)

    t, r = grid(128)
    j, td = t % W, t // W
    zt = td // 2 % NZ
    gt = 2 * (td // (2 * NZ)) + td % 2
    live = j < count_t
    place = before + j
    packed = step_t * 32 + place
    key = row * W + shift_t
    by_rank = (start + place == r) & live
    rank_packed = gather(by_rank, packed)
    rank_key = gather(by_rank, key)
    mu, w = rank_key // W, rank_key % W

    def block_place(b):
        return (2 * (b // (2 * NZ)) + b % 2) * NZ + b // 2 % NZ

    tab[0:1, :] = rank_packed
    tab[1:2, :] = block_place(mu)
    for n in range(3):
        near_w = w + 1 - n
        near_key = ((mu + RANKS + n - 1) % RANKS) * W + near_w
        match = (key == near_key) & live & (near_w >= 0) & (near_w < W)
        found = gather(match, packed + 1)
        tab[2 + n : 3 + n, :] = jnp.where(found > 0, found - 1, rank_packed)
        tab[5 + n : 6 + n, :] = jnp.where(found > 0, 1, 0)
    in_plane = (zt == z) & live
    hit = in_plane & (place == r)
    tab[8:9, :] = gather(hit, gt * W + j)
    spare = r[0:1, :] >= gather(in_plane, 1)
    first = gather(in_plane & (place == 0), shift_t)
    tab[9:10, :] = gather(hit, gt * W + shift_t) + jnp.where(spare, first, 0)
    own = td == pi
    own_row = gather(own & (j == 0), row)
    tab[10:11, :] = block_place((own_row + RANKS + r[0:1, :] - 2) % RANKS)
    tab[11:12, :] = gather(own & live & (shift_t == r), 1)
    tab[12:13, :] = jnp.minimum(gather(own & (shift_t == r), j), W - 1)
    tab[13:16, :] = jnp.zeros((3, 128), jnp.int32)


def kernel(
    cap,
    part,
    count_v,
    owner_v,
    shift_v,
    virt_v,
    occ_v,
    tnat_h,
    out,
    tab_v,
    tab,
    tnat,
    ts,
    comb,
    hs,
    hbuf,
    txr0, txr1, txr2, txr3, txr4, txr5, txr6, txr7,
    hxr0, hxr1, hxr2, hxr3, hxr4, hxr5, hxr6, hxr7,
    tc,
    hc,
    tza,
    tzb,
    hz,
    at1,
    at2,
    fbuf,
    fout,
    pbuf,
    prx,
    rxs,
    rxr,
    rzs,
    rzr,
    sems,
    txr_s,
    tzr_s,
    hxr_s,
    hzr_s,
    ys_s,
    yr_s,
    cs_s,
    cr_s,
    loc_s,
    own_s,
    out_s,
    ps_s,
    pr_s,
    xs_s,
    xr_s,
    sw_s,
):
    txr = (txr0, txr1, txr2, txr3, txr4, txr5, txr6, txr7)
    hxr = (hxr0, hxr1, hxr2, hxr3, hxr4, hxr5, hxr6, hxr7)
    pi = lax.axis_index("pair")
    y = lax.axis_index("aux")
    c = pi % 2
    z = pi // 2 % NZ
    x = pi // (2 * NZ)
    g = 2 * x + c

    def dev_g(gg):
        return ((gg // 2 * NZ + z) * 2 + gg % 2, y)

    def dev_z(zz):
        return ((x * NZ + zz) * 2 + c, y)

    yp, ym = (y + 1) % NY, (y + NY - 1) % NY
    core = dev_g(g + 1 - 2 * c)

    def remote(src, dst, send, recv, device):
        return pltpu.make_async_remote_copy(
            src_ref=src, dst_ref=dst, send_sem=send, recv_sem=recv, device_id=device, device_id_type=MESH
        )

    def wait_bytes(ref, sem):
        pltpu.make_async_copy(ref, ref, sem).wait()

    barrier = pltpu.get_barrier_semaphore()
    for i in range(1, NG):
        pl.semaphore_signal(barrier, inc=1, device_id=dev_g((g + i) % NG), device_id_type=MESH)
    for i in range(1, NZ):
        pl.semaphore_signal(barrier, inc=1, device_id=dev_z((z + i) % NZ), device_id_type=MESH)
    pl.semaphore_signal(barrier, inc=1, device_id=(pi, yp), device_id_type=MESH)
    pl.semaphore_signal(barrier, inc=1, device_id=(pi, ym), device_id_type=MESH)

    own_t, own_h = [], []
    nat = pltpu.make_async_copy(tnat_h, tnat, loc_s.at[1])
    nat.start()
    gap = jnp.zeros((TB, TB), BF)
    blocks = [virt_v[0, i] for i in range(7)] + [gap] + [occ_v[0, i] for i in range(3)] + [gap]
    comb[g * NZ + z] = jnp.concatenate(blocks, axis=1)
    nat.wait()

    def split(st):
        @pl.loop(0, W)
        def _(j):
            for mh in range(2):
                for q in range(0, QL, 128):
                    part = tnat[j, mh * HB : (mh + 1) * HB, pl.ds(pl.multiple_of(st * HB, HB), HB), q : q + 128]
                    part = jnp.swapaxes(part.astype(F32), 0, 1).astype(BF)
                    ts[pl.ds(st * HB, HB), j, mh * HB : (mh + 1) * HB, q : q + 128] = part

    first = (z + OFF[0]) % NZ // (NZ // 2)
    split(first)
    pl.semaphore_wait(barrier, NG + NZ)

    for i in range(1, NZ):
        remote(comb.at[g * NZ + z], comb.at[g * NZ + z], cs_s.at[0], cr_s.at[0], dev_z((z + i) % NZ)).start()

    def t_send(k):
        zb = (z + OFF[k]) % NZ
        own_t.append(
            pltpu.make_async_copy(
                ts.at[zb * NX + x, :, pl.ds(HB * c, HB), :], txr[k].at[pl.ds(W * g, W)], own_s.at[k]
            )
        )
        own_t[k].start()
        for i in range(1, NG):
            gg = (g + i) % NG
            remote(
                ts.at[zb * NX + gg // 2, :, pl.ds(HB * (gg % 2), HB), :],
                txr[k].at[pl.ds(W * g, W)],
                out_s.at[k],
                txr_s.at[k],
                dev_g(gg),
            ).start()

    t_send(0)
    split(1 - first)
    for k in range(1, AHEAD):
        t_send(k)

    fill_tables(pi, z, count_v[...], owner_v[...], shift_v[...], tab_v)
    tab_c = pltpu.make_async_copy(tab_v, tab, loc_s.at[0])
    tab_c.start()
    tab_c.wait()

    def tz_at(k):
        return tza.at[k] if k < NA else tzb.at[k - NA]

    def t_step(k):
        zb = (z + OFF[k]) % NZ
        own_t[k].wait()
        wait_bytes(txr[k].at[pl.ds(0, (NG - 1) * W)], txr_s.at[k])
        if k + AHEAD < NZ:
            t_send(k + AHEAD)
        if OFF[k] == 0:

            @pl.loop(0, cap)
            def _(i):
                tzb[k - NA, i] = txr[k][tab[8, i]]

        else:

            @pl.loop(0, cap)
            def _(i):
                tc[k, i] = txr[k][tab[8, i]]

            remote(tc.at[k], tz_at(k), sems.at[1], tzr_s.at[k], dev_z(zb)).start()

    t_step(0)
    t_step(1)
    wait_bytes(comb.at[pl.ds(0, NZ - 1)], cr_s.at[0])
    for i in range(1, NX):
        remote(
            comb.at[pl.ds(g * NZ, NZ)], comb.at[pl.ds(g * NZ, NZ)], cs_s.at[1], cr_s.at[1], dev_g((g + 2 * i) % NG)
        ).start()
    remote(comb.at[pl.ds(g * NZ, NZ)], comb.at[pl.ds(g * NZ, NZ)], cs_s.at[1], cr_s.at[1], core).start()
    t_step(2)
    t_step(3)
    wait_bytes(comb.at[pl.ds(0, NX * NZ)], cr_s.at[1])
    for i in range(1, NX):
        gg = (g + 2 * i) % NG
        remote(comb.at[pl.ds(gg * NZ, NZ)], comb.at[pl.ds(gg * NZ, NZ)], cs_s.at[2], cr_s.at[2], core).start()
    t_step(4)

    wait_bytes(comb.at[pl.ds(0, (NX - 1) * NZ)], cr_s.at[2])
    lane = lax.broadcasted_iota(jnp.int32, (TB, W * TB), 1) // TB
    keep = lane < 0
    for kk in range(W):
        keep = keep | ((lane == kk) & (tab[11, kk] > 0))
    rows = []
    for ww in range(W):
        band = comb[tab[10, ww], :, 0:256].astype(F32)
        band = pltpu.roll(band, (256 - TB * (W - 1 - ww)) % 256, 1)[:, : W * TB]
        rows.append(jnp.where(keep, band, 0.0).astype(BF))
    vmat = jnp.concatenate(rows, axis=0)
    slots = [tab[12, ww] for ww in range(W)]

    def h_form(qh, mh):
        @pl.loop(0, HB)
        def _(mi):
            rhs = jnp.concatenate(
                [tnat[slots[ww], mh * HB + mi, :, qh * QH : (qh + 1) * QH] for ww in range(W)], axis=0
            )
            hs[mi] = jnp.dot(vmat, rhs, preferred_element_type=F32)

        for ww in range(W):

            @pl.loop(0, TB // 8)
            def _(sb):
                part = hs[:, pl.ds(ww * TB + sb * 8, 8), :]
                hbuf[qh, pl.ds(sb * 8, 8), ww, mh * HB : (mh + 1) * HB, :] = jnp.swapaxes(part, 0, 1).astype(BF)

    h_form(0, 0)
    h_form(0, 1)
    t_step(5)
    h_form(1, 0)
    t_step(6)
    h_form(1, 1)

    def h_send(k):
        zb = (z + OFF[k]) % NZ
        own_h.append(pltpu.make_async_copy(hbuf.at[c, zb * NX + x], hxr[k].at[pl.ds(W * g, W)], own_s.at[NZ + k]))
        own_h[k].start()
        for i in range(1, NG):
            gg = (g + i) % NG
            remote(
                hbuf.at[gg % 2, zb * NX + gg // 2], hxr[k].at[pl.ds(W * g, W)], out_s.at[NZ + k], hxr_s.at[k], dev_g(gg)
            ).start()

    h_send(0)
    t_step(7)
    for k in range(1, AHEAD):
        h_send(k)

    def turn(buf, begin, end, tile):
        @pl.loop(begin // 8, end // 8)
        def _(b):
            tiles = [tile(tab[0, b * 8 + i]) for i in range(8)]
            place = pl.ds(pl.multiple_of((b - begin // 8) * 128, 128), 128)
            buf[y, :, place] = jnp.concatenate(tiles, axis=0).T

    lo, hi = pl.ds(0, QH), pl.ds(QH, QH)
    y2 = (y + 2) % NY

    def spread(buf, s0):
        remote(buf.at[y, lo], buf.at[y, lo], ys_s.at[s0], yr_s.at[s0], (pi, yp)).start()
        remote(buf.at[y, hi], buf.at[y, hi], ys_s.at[s0 + 1], yr_s.at[s0 + 1], (pi, ym)).start()
        remote(buf.at[y, hi], buf.at[y, hi], ys_s.at[s0 + 2], yr_s.at[s0 + 2], (pi, yp)).start()
        remote(buf.at[y, lo], buf.at[y, lo], ys_s.at[s0 + 3], yr_s.at[s0 + 3], (pi, ym)).start()

    def forward(buf, s0):
        wait_bytes(buf.at[ym, lo], yr_s.at[s0])
        remote(buf.at[ym, lo], buf.at[ym, lo], ys_s.at[s0 + 4], yr_s.at[s0 + 4], (pi, yp)).start()
        wait_bytes(buf.at[yp, hi], yr_s.at[s0 + 1])
        remote(buf.at[yp, hi], buf.at[yp, hi], ys_s.at[s0 + 5], yr_s.at[s0 + 5], (pi, ym)).start()

    def near_tile(p):
        return tza[p // 32, p % 32]

    def any_tile(p):
        step = p // 32
        early = tza[jnp.minimum(step, NA - 1), p % 32]
        late = tzb[jnp.maximum(step - NA, 0), p % 32]
        return jnp.where(step < NA, early, late)

    for k in range(NA):
        wait_bytes(tz_at(k), tzr_s.at[k])
    turn(at1, 0, part, near_tile)
    spread(at1, 0)

    def h_step(k):
        zb = (z + OFF[k]) % NZ
        own_h[k].wait()
        wait_bytes(hxr[k].at[pl.ds(0, (NG - 1) * W)], hxr_s.at[k])
        if k + AHEAD < NZ:
            h_send(k + AHEAD)
        if OFF[k] == 0:

            @pl.loop(0, cap)
            def _(i):
                hz[k, i] = hxr[k][tab[9, i]]

        else:

            @pl.loop(0, cap)
            def _(i):
                hc[k, i] = hxr[k][tab[9, i]]

            remote(hc.at[k], hz.at[k], sems.at[3], hzr_s.at[k], dev_z(zb)).start()

    h_step(0)
    h_step(1)
    forward(at1, 0)
    for k in range(NA, NZ - 1):
        wait_bytes(tz_at(k), tzr_s.at[k])
    turn(at2, part, LIVE, any_tile)
    spread(at2, 6)
    for k in range(2, 6):
        h_step(k)
    forward(at2, 6)
    h_step(6)
    h_step(7)

    for k in range(NZ - 1):
        wait_bytes(hz.at[k], hzr_s.at[k])
    lane3 = lax.broadcasted_iota(jnp.int32, (TB, 3 * TB), 1) // TB
    lower = c == 0
    swaps = []
    for q in range(4):
        span = pl.ds(q * (LIVE // 4), LIVE // 4)

        @pl.loop(q * (LIVE // 4), (q + 1) * (LIVE // 4), unroll=4)
        def _(t):
            occ = comb[tab[1, t], :, 256 : 256 + 3 * TB]
            src, use = [], lane3 < 0
            for r in range(3):
                p = tab[2 + r, t]
                src.append(hz[p // 32, p % 32])
                use = use | ((lane3 == r) & (tab[5 + r, t] > 0))
            occ = jnp.where(use, occ.astype(F32), 0.0).astype(BF)
            f = jnp.dot(occ, jnp.concatenate(src, axis=0), preferred_element_type=F32).astype(BF)
            fbuf[c, t] = jnp.where(lower, f[:HB], f[HB:])
            fout[t] = jnp.where(lower, f[HB:], f[:HB])

        swaps.append(remote(fout.at[span], fbuf.at[c, span], sw_s.at[q], sw_s.at[4 + q], core))
        swaps[q].start()
    for buf, s0 in ((at1, 0), (at2, 6)):
        for i, ref in ((2, buf.at[ym, hi]), (3, buf.at[yp, lo]), (4, buf.at[y2, lo]), (5, buf.at[y2, hi])):
            wait_bytes(ref, yr_s.at[s0 + i])
    for swap in swaps:
        swap.wait_recv()

    def core_sum(h, i):
        xb = (x + 1 + i) % NX
        wait_bytes(prx.at[h, i], pr_s.at[NX * h + i])
        return pbuf[h, xb, :, c] + prx[h, i]

    def ship(h, i):
        xb = (x + 1 + i) % NX
        rxs[h, i] = core_sum(h, i).astype(BF)
        remote(rxs.at[h, i], rxr.at[h, i], xs_s.at[NX * h + i], xr_s.at[NX * h + i], dev_g(2 * xb + c)).start()

    for h in range(2):
        for i in range(NX):
            xb = (x + 1 + i) % NX

            @pl.loop(0, 4)
            def _(mt):
                rows = pl.ds(mt * 128, 128)
                early, late = fbuf[h, :part].reshape(part * HB, QH), fbuf[h, part:].reshape((LIVE - part) * HB, QH)
                term = jnp.dot(at1[xb, rows, :], early, preferred_element_type=F32)
                term = term + jnp.dot(at2[xb, rows, :], late, preferred_element_type=F32)
                pbuf[h, xb, pl.ds(mt * 2, 2)] = term.reshape(2, 2, TB, QH)

            remote(pbuf.at[h, xb, :, 1 - c], prx.at[h, i], ps_s.at[NX * h + i], pr_s.at[NX * h + i], core).start()
            if i > 0:
                ship(h, i - 1)

    for h in range(2):
        total = core_sum(h, NX - 1)
        for i in range(NX - 1):
            wait_bytes(rxr.at[h, i], xr_s.at[NX * h + i])
            total = total + rxr[h, i].astype(F32)
        rzs[h] = total.astype(BF)
        for i in range(1, NZ):
            zz = (z + i) % NZ
            remote(rzs.at[h, zz], rzr.at[h, z], sems.at[6 + h], sems.at[8 + h], dev_z(zz)).start()
        rzr[h, z] = rzs[h, z]
    for h in range(2):
        wait_bytes(rzs.at[h, pl.ds(0, NZ - 1)], sems.at[8 + h])
        final = rzr[h, 0].astype(F32)
        for zz in range(1, NZ):
            final = final + rzr[h, zz].astype(F32)
        out[:, h * QH : (h + 1) * QH] = final * (1.0 / math.sqrt(TB * TB * LIVE))

    wait_bytes(comb.at[pl.ds(0, NZ - 1)], cs_s.at[0])
    wait_bytes(comb.at[pl.ds(0, NX * NZ)], cs_s.at[1])
    wait_bytes(comb.at[pl.ds(0, (NX - 1) * NZ)], cs_s.at[2])
    for k in range(NZ):
        wait_bytes(txr[k].at[pl.ds(0, (NG - 1) * W)], out_s.at[k])
    wait_bytes(tc.at[pl.ds(0, NZ - 1)], sems.at[1])
    for k in range(NZ):
        wait_bytes(hxr[k].at[pl.ds(0, (NG - 1) * W)], out_s.at[NZ + k])
    wait_bytes(hc.at[pl.ds(0, NZ - 1)], sems.at[3])
    for swap in swaps:
        swap.wait_send()
    for i in range(6):
        wait_bytes(at1.at[y, lo], ys_s.at[i])
        wait_bytes(at2.at[y, lo], ys_s.at[6 + i])
    for h in range(2):
        wait_bytes(rzs.at[h, pl.ds(0, NZ - 1)], sems.at[6 + h])
        for i in range(NX - 1):
            wait_bytes(rxs.at[h, i], xs_s.at[NX * h + i])
        for i in range(NX):
            wait_bytes(prx.at[h, i], ps_s.at[NX * h + i])


def fused(cap, part, cid, *operands):
    vmem = pl.BlockSpec(memory_space=pltpu.VMEM)
    hbm = pl.BlockSpec(memory_space=pl.ANY)
    dma = pltpu.SemaphoreType.DMA
    return pl.pallas_call(
        functools.partial(kernel, cap, part),
        out_shape=jax.ShapeDtypeStruct((TB, QL), F32),
        in_specs=[vmem] * 5 + [hbm],
        out_specs=vmem,
        scratch_shapes=[
            pltpu.VMEM((16, 128), jnp.int32),
            pltpu.SMEM((16, 128), jnp.int32),
            pltpu.VMEM((W, TB, TB, QL), BF),
            pltpu.VMEM((TB, W, TB, QL), BF),
            pltpu.VMEM((RANKS, TB, 384), BF),
            pltpu.VMEM((HB, W * TB, QH), F32),
            pltpu.VMEM((2, TB, W, TB, QH), BF),
        ]
        + [pltpu.VMEM((NG * W, HB, QL), BF)] * NZ
        + [pltpu.VMEM((NG * W, TB, QH), BF)] * NZ
        + [
            pltpu.VMEM((NZ, cap, HB, QL), BF),
            pltpu.VMEM((NZ, cap, TB, QH), BF),
            pltpu.VMEM((NA, cap, HB, QL), BF),
            pltpu.VMEM((NZ - NA, cap, HB, QL), BF),
            pltpu.VMEM((NZ, cap, TB, QH), BF),
            pltpu.VMEM((NY, QL, part * HB), BF),
            pltpu.VMEM((NY, QL, (LIVE - part) * HB), BF),
            pltpu.VMEM((2, LIVE, HB, QH), BF),
            pltpu.VMEM((LIVE, HB, QH), BF),
            pltpu.VMEM((2, NX, NZ, 2, TB, QH), F32),
            pltpu.VMEM((2, NX, NZ, TB, QH), F32),
            pltpu.VMEM((2, NX - 1, NZ, TB, QH), BF),
            pltpu.VMEM((2, NX - 1, NZ, TB, QH), BF),
            pltpu.VMEM((2, NZ, TB, QH), BF),
            pltpu.VMEM((2, NZ, TB, QH), BF),
            dma((10,)),
            dma((NZ,)),
            dma((NZ,)),
            dma((NZ,)),
            dma((NZ,)),
            dma((12,)),
            dma((12,)),
            dma((3,)),
            dma((3,)),
            dma((4,)),
            dma((2 * NZ,)),
            dma((2 * NZ,)),
            dma((2 * NX,)),
            dma((2 * NX,)),
            dma((2 * NX,)),
            dma((2 * NX,)),
            dma((8,)),
        ],
        compiler_params=pltpu.CompilerParams(
            collective_id=cid, has_side_effects=True, vmem_limit_bytes=62 * 2**20
        ),
    )(*operands)


def per_device(three_index, occ_blocks, virt_blocks, tile_shift, tile_count, block_owner):
    plane_of = np.arange(RANKS) // 2 % NZ
    planes = np.arange(NZ)[:, None]
    early = np.isin((planes - plane_of) % NZ, OFF[:NA])
    chosen = np.concatenate([planes == plane_of, early]).astype(np.int32)
    tiles = jnp.sum(tile_count[None, :] * chosen, axis=1)
    is_plane = np.arange(2 * NZ) < NZ
    need = jnp.where(is_plane | (tiles >= SIZES[0][1]), 0, len(SIZES) - 1)
    for cap, _ in SIZES[:-1]:
        need = need + jnp.where(is_plane & (tiles > cap), 1, 0)
    return lax.switch(
        jnp.max(need),
        [functools.partial(fused, cap, part, 1 + i) for i, (cap, part) in enumerate(SIZES)],
        tile_count.reshape(1, RANKS),
        block_owner.reshape(1, RANKS),
        tile_shift,
        virt_blocks,
        occ_blocks,
        three_index,
    )


def solution(mesh):
    in_specs = (
        P("pair", None, None, "aux"),
        P("pair", None, None, None),
        P("pair", None, None, None),
        P(),
        P(),
        P(),
    )
    return jax.shard_map(per_device, mesh=mesh, in_specs=in_specs, out_specs=P("pair", "aux"), check_vma=False)
```

```python
import functools
import math

import jax
import jax.numpy as jnp
import numpy as np
from jax import lax
from jax.experimental import pallas as pl
from jax.experimental.pallas import tpu as pltpu
from jax.sharding import PartitionSpec as P

NX, NY, NZ = 4, 4, 8
NG = 2 * NX
W = 4
TB = 32
HB = TB // 2
QL = 512
QH = QL // 2
LIVE = 128
RANKS = NG * NZ
OFF = (4, 3, 5, 2, 6, 1, 7, 0)
NA = 3
AHEAD = 2
SIZES = ((19, 32), (20, 32), (21, 32), (23, 32), (32, 24))
MESH = pl.DeviceIdType.MESH
BF, F32 = jnp.bfloat16, jnp.float32


def fill_tables(pi, z, count, owner, shift, tab):
    tiles = RANKS * W

    def grid(lanes):
        return lax.broadcasted_iota(jnp.int32, (tiles, lanes), 0), lax.broadcasted_iota(jnp.int32, (tiles, lanes), 1)

    def pick(cond, value):
        return jnp.sum(jnp.where(cond, value, 0), axis=1, keepdims=True)

    def gather(cond, value):
        return jnp.sum(jnp.where(cond, value, 0), axis=0, keepdims=True)

    t, d = grid(RANKS)
    td = t // W
    zt, zd = td // 2 % NZ, d // 2 % NZ

    def step_of(plane):
        away = (z + NZ - plane) % NZ
        return sum(jnp.where(away == OFF[k], k, 0) for k in range(NZ))

    step_t = step_of(zt)
    count_t = pick(d == td, count)
    before = pick((zd == zt) & (d < td), count)
    start = pick(step_of(zd) < step_t, count)
    row = pick(owner == td, d)
    step_t = step_t[:, 0:1]
    tt, lane = grid(tiles)
    sub = lax.broadcasted_iota(jnp.int32, (RANKS, tiles), 0)
    at_lane = lax.broadcasted_iota(jnp.int32, (RANKS, tiles), 1)
    shift_r = jnp.zeros((1, tiles), jnp.int32)
    for jj in range(W):
        shift_r = shift_r + gather((at_lane // W == sub) & (at_lane % W == jj), shift[:, jj : jj + 1])
    shift_t = pick(tt == lane, shift_r)

    t, r = grid(128)
    j, td = t % W, t // W
    zt = td // 2 % NZ
    gt = 2 * (td // (2 * NZ)) + td % 2
    live = j < count_t
    place = before + j
    packed = step_t * 32 + place
    key = row * W + shift_t
    by_rank = (start + place == r) & live
    rank_packed = gather(by_rank, packed)
    rank_key = gather(by_rank, key)
    mu, w = rank_key // W, rank_key % W

    def block_place(b):
        return (2 * (b // (2 * NZ)) + b % 2) * NZ + b // 2 % NZ

    tab[0:1, :] = rank_packed
    tab[1:2, :] = block_place(mu)
    for n in range(3):
        near_w = w + 1 - n
        near_key = ((mu + RANKS + n - 1) % RANKS) * W + near_w
        match = (key == near_key) & live & (near_w >= 0) & (near_w < W)
        found = gather(match, packed + 1)
        tab[2 + n : 3 + n, :] = jnp.where(found > 0, found - 1, rank_packed)
        tab[5 + n : 6 + n, :] = jnp.where(found > 0, 1, 0)
    in_plane = (zt == z) & live
    hit = in_plane & (place == r)
    tab[8:9, :] = gather(hit, gt * W + j)
    spare = r[0:1, :] >= gather(in_plane, 1)
    first = gather(in_plane & (place == 0), shift_t)
    tab[9:10, :] = gather(hit, gt * W + shift_t) + jnp.where(spare, first, 0)
    own = td == pi
    own_row = gather(own & (j == 0), row)
    tab[10:11, :] = block_place((own_row + RANKS + r[0:1, :] - 2) % RANKS)
    tab[11:12, :] = gather(own & live & (shift_t == r), 1)
    tab[12:13, :] = jnp.minimum(gather(own & (shift_t == r), j), W - 1)
    tab[13:16, :] = jnp.zeros((3, 128), jnp.int32)


def kernel(
    cap,
    part,
    count_v,
    owner_v,
    shift_v,
    virt_v,
    occ_v,
    tnat_h,
    out,
    tab_v,
    tab,
    tnat,
    ts,
    comb,
    hs,
    hbuf,
    txr0, txr1, txr2, txr3, txr4, txr5, txr6, txr7,
    hxr0, hxr1, hxr2, hxr3, hxr4, hxr5, hxr6, hxr7,
    tc,
    hc,
    tza,
    tzb,
    hz,
    at1,
    at2,
    fbuf,
    fout,
    pbuf,
    prx,
    rxs,
    rxr,
    rzs,
    rzr,
    sems,
    txr_s,
    tzr_s,
    hxr_s,
    hzr_s,
    ys_s,
    yr_s,
    cs_s,
    cr_s,
    loc_s,
    own_s,
    out_s,
    ps_s,
    pr_s,
    xs_s,
    xr_s,
    sw_s,
):
    txr = (txr0, txr1, txr2, txr3, txr4, txr5, txr6, txr7)
    hxr = (hxr0, hxr1, hxr2, hxr3, hxr4, hxr5, hxr6, hxr7)
    pi = lax.axis_index("pair")
    y = lax.axis_index("aux")
    c = pi % 2
    z = pi // 2 % NZ
    x = pi // (2 * NZ)
    g = 2 * x + c

    def dev_g(gg):
        return ((gg // 2 * NZ + z) * 2 + gg % 2, y)

    def dev_z(zz):
        return ((x * NZ + zz) * 2 + c, y)

    yp, ym = (y + 1) % NY, (y + NY - 1) % NY
    core = dev_g(g + 1 - 2 * c)

    def remote(src, dst, send, recv, device):
        return pltpu.make_async_remote_copy(
            src_ref=src, dst_ref=dst, send_sem=send, recv_sem=recv, device_id=device, device_id_type=MESH
        )

    def wait_bytes(ref, sem):
        pltpu.make_async_copy(ref, ref, sem).wait()

    barrier = pltpu.get_barrier_semaphore()
    for i in range(1, NG):
        pl.semaphore_signal(barrier, inc=1, device_id=dev_g((g + i) % NG), device_id_type=MESH)
    for i in range(1, NZ):
        pl.semaphore_signal(barrier, inc=1, device_id=dev_z((z + i) % NZ), device_id_type=MESH)
    pl.semaphore_signal(barrier, inc=1, device_id=(pi, yp), device_id_type=MESH)
    pl.semaphore_signal(barrier, inc=1, device_id=(pi, ym), device_id_type=MESH)

    own_t, own_h = [], []
    nat = pltpu.make_async_copy(tnat_h, tnat, loc_s.at[1])
    nat.start()
    gap = jnp.zeros((TB, TB), BF)
    blocks = [virt_v[0, i] for i in range(7)] + [gap] + [occ_v[0, i] for i in range(3)] + [gap]
    comb[g * NZ + z] = jnp.concatenate(blocks, axis=1)
    nat.wait()

    def split(st):
        @pl.loop(0, W)
        def _(j):
            for mh in range(2):
                for q in range(0, QL, 128):
                    part = tnat[j, mh * HB : (mh + 1) * HB, pl.ds(pl.multiple_of(st * HB, HB), HB), q : q + 128]
                    part = jnp.swapaxes(part.astype(F32), 0, 1).astype(BF)
                    ts[pl.ds(st * HB, HB), j, mh * HB : (mh + 1) * HB, q : q + 128] = part

    first = (z + OFF[0]) % NZ // (NZ // 2)
    split(first)
    pl.semaphore_wait(barrier, NG + NZ)

    for i in range(1, NZ):
        remote(comb.at[g * NZ + z], comb.at[g * NZ + z], cs_s.at[0], cr_s.at[0], dev_z((z + i) % NZ)).start()

    def t_send(k):
        zb = (z + OFF[k]) % NZ
        own_t.append(
            pltpu.make_async_copy(
                ts.at[zb * NX + x, :, pl.ds(HB * c, HB), :], txr[k].at[pl.ds(W * g, W)], own_s.at[k]
            )
        )
        own_t[k].start()
        for i in range(1, NG):
            gg = (g + i) % NG
            remote(
                ts.at[zb * NX + gg // 2, :, pl.ds(HB * (gg % 2), HB), :],
                txr[k].at[pl.ds(W * g, W)],
                out_s.at[k],
                txr_s.at[k],
                dev_g(gg),
            ).start()

    t_send(0)
    split(1 - first)
    for k in range(1, AHEAD):
        t_send(k)

    fill_tables(pi, z, count_v[...], owner_v[...], shift_v[...], tab_v)
    tab_c = pltpu.make_async_copy(tab_v, tab, loc_s.at[0])
    tab_c.start()
    tab_c.wait()

    def tz_at(k):
        return tza.at[k] if k < NA else tzb.at[k - NA]

    def t_step(k):
        zb = (z + OFF[k]) % NZ
        own_t[k].wait()
        wait_bytes(txr[k].at[pl.ds(0, (NG - 1) * W)], txr_s.at[k])
        if k + AHEAD < NZ:
            t_send(k + AHEAD)
        if OFF[k] == 0:

            @pl.loop(0, cap)
            def _(i):
                tzb[k - NA, i] = txr[k][tab[8, i]]

        else:

            @pl.loop(0, cap)
            def _(i):
                tc[k, i] = txr[k][tab[8, i]]

            remote(tc.at[k], tz_at(k), sems.at[1], tzr_s.at[k], dev_z(zb)).start()

    t_step(0)
    t_step(1)
    wait_bytes(comb.at[pl.ds(0, NZ - 1)], cr_s.at[0])
    for i in range(1, NX):
        remote(
            comb.at[pl.ds(g * NZ, NZ)], comb.at[pl.ds(g * NZ, NZ)], cs_s.at[1], cr_s.at[1], dev_g((g + 2 * i) % NG)
        ).start()
    remote(comb.at[pl.ds(g * NZ, NZ)], comb.at[pl.ds(g * NZ, NZ)], cs_s.at[1], cr_s.at[1], core).start()
    t_step(2)
    t_step(3)
    wait_bytes(comb.at[pl.ds(0, NX * NZ)], cr_s.at[1])
    for i in range(1, NX):
        gg = (g + 2 * i) % NG
        remote(comb.at[pl.ds(gg * NZ, NZ)], comb.at[pl.ds(gg * NZ, NZ)], cs_s.at[2], cr_s.at[2], core).start()
    t_step(4)

    wait_bytes(comb.at[pl.ds(0, (NX - 1) * NZ)], cr_s.at[2])
    lane = lax.broadcasted_iota(jnp.int32, (TB, W * TB), 1) // TB
    keep = lane < 0
    for kk in range(W):
        keep = keep | ((lane == kk) & (tab[11, kk] > 0))
    rows = []
    for ww in range(W):
        band = comb[tab[10, ww], :, 0:256].astype(F32)
        band = pltpu.roll(band, (256 - TB * (W - 1 - ww)) % 256, 1)[:, : W * TB]
        rows.append(jnp.where(keep, band, 0.0).astype(BF))
    vmat = jnp.concatenate(rows, axis=0)
    slots = [tab[12, ww] for ww in range(W)]

    def h_form(qh, mh):
        @pl.loop(0, HB)
        def _(mi):
            rhs = jnp.concatenate(
                [tnat[slots[ww], mh * HB + mi, :, qh * QH : (qh + 1) * QH] for ww in range(W)], axis=0
            )
            hs[mi] = jnp.dot(vmat, rhs, preferred_element_type=F32)

        for ww in range(W):

            @pl.loop(0, TB // 8)
            def _(sb):
                part = hs[:, pl.ds(ww * TB + sb * 8, 8), :]
                hbuf[qh, pl.ds(sb * 8, 8), ww, mh * HB : (mh + 1) * HB, :] = jnp.swapaxes(part, 0, 1).astype(BF)

    h_form(0, 0)
    h_form(0, 1)
    t_step(5)
    h_form(1, 0)
    t_step(6)
    h_form(1, 1)

    def h_send(k):
        zb = (z + OFF[k]) % NZ
        own_h.append(pltpu.make_async_copy(hbuf.at[c, zb * NX + x], hxr[k].at[pl.ds(W * g, W)], own_s.at[NZ + k]))
        own_h[k].start()
        for i in range(1, NG):
            gg = (g + i) % NG
            remote(
                hbuf.at[gg % 2, zb * NX + gg // 2], hxr[k].at[pl.ds(W * g, W)], out_s.at[NZ + k], hxr_s.at[k], dev_g(gg)
            ).start()

    h_send(0)
    t_step(7)
    for k in range(1, AHEAD):
        h_send(k)

    def turn(buf, begin, end, tile):
        @pl.loop(begin // 8, end // 8)
        def _(b):
            tiles = [tile(tab[0, b * 8 + i]) for i in range(8)]
            place = pl.ds(pl.multiple_of((b - begin // 8) * 128, 128), 128)
            buf[y, :, place] = jnp.concatenate(tiles, axis=0).T

    lo, hi = pl.ds(0, QH), pl.ds(QH, QH)
    y2 = (y + 2) % NY

    def spread(buf, s0):
        remote(buf.at[y, lo], buf.at[y, lo], ys_s.at[s0], yr_s.at[s0], (pi, yp)).start()
        remote(buf.at[y, hi], buf.at[y, hi], ys_s.at[s0 + 1], yr_s.at[s0 + 1], (pi, ym)).start()
        remote(buf.at[y, hi], buf.at[y, hi], ys_s.at[s0 + 2], yr_s.at[s0 + 2], (pi, yp)).start()
        remote(buf.at[y, lo], buf.at[y, lo], ys_s.at[s0 + 3], yr_s.at[s0 + 3], (pi, ym)).start()

    def forward(buf, s0):
        wait_bytes(buf.at[ym, lo], yr_s.at[s0])
        remote(buf.at[ym, lo], buf.at[ym, lo], ys_s.at[s0 + 4], yr_s.at[s0 + 4], (pi, yp)).start()
        wait_bytes(buf.at[yp, hi], yr_s.at[s0 + 1])
        remote(buf.at[yp, hi], buf.at[yp, hi], ys_s.at[s0 + 5], yr_s.at[s0 + 5], (pi, ym)).start()

    def near_tile(p):
        return tza[p // 32, p % 32]

    def any_tile(p):
        step = p // 32
        early = tza[jnp.minimum(step, NA - 1), p % 32]
        late = tzb[jnp.maximum(step - NA, 0), p % 32]
        return jnp.where(step < NA, early, late)

    for k in range(NA):
        wait_bytes(tz_at(k), tzr_s.at[k])
    turn(at1, 0, part, near_tile)
    spread(at1, 0)

    def h_step(k):
        zb = (z + OFF[k]) % NZ
        own_h[k].wait()
        wait_bytes(hxr[k].at[pl.ds(0, (NG - 1) * W)], hxr_s.at[k])
        if k + AHEAD < NZ:
            h_send(k + AHEAD)
        if OFF[k] == 0:

            @pl.loop(0, cap)
            def _(i):
                hz[k, i] = hxr[k][tab[9, i]]

        else:

            @pl.loop(0, cap)
            def _(i):
                hc[k, i] = hxr[k][tab[9, i]]

            remote(hc.at[k], hz.at[k], sems.at[3], hzr_s.at[k], dev_z(zb)).start()

    h_step(0)
    h_step(1)
    forward(at1, 0)
    for k in range(NA, NZ - 1):
        wait_bytes(tz_at(k), tzr_s.at[k])
    turn(at2, part, LIVE, any_tile)
    spread(at2, 6)
    for k in range(2, 6):
        h_step(k)
    forward(at2, 6)
    h_step(6)
    h_step(7)

    for k in range(NZ - 1):
        wait_bytes(hz.at[k], hzr_s.at[k])
    lane3 = lax.broadcasted_iota(jnp.int32, (TB, 3 * TB), 1) // TB
    lower = c == 0
    swaps = []
    for q in range(4):
        span = pl.ds(q * (LIVE // 4), LIVE // 4)

        @pl.loop(q * (LIVE // 4), (q + 1) * (LIVE // 4), unroll=4)
        def _(t):
            occ = comb[tab[1, t], :, 256 : 256 + 3 * TB]
            src, use = [], lane3 < 0
            for r in range(3):
                p = tab[2 + r, t]
                src.append(hz[p // 32, p % 32])
                use = use | ((lane3 == r) & (tab[5 + r, t] > 0))
            occ = jnp.where(use, occ.astype(F32), 0.0).astype(BF)
            f = jnp.dot(occ, jnp.concatenate(src, axis=0), preferred_element_type=F32).astype(BF)
            fbuf[c, t] = jnp.where(lower, f[:HB], f[HB:])
            fout[t] = jnp.where(lower, f[HB:], f[:HB])

        swaps.append(remote(fout.at[span], fbuf.at[c, span], sw_s.at[q], sw_s.at[4 + q], core))
        swaps[q].start()
    for buf, s0 in ((at1, 0), (at2, 6)):
        for i, ref in ((2, buf.at[ym, hi]), (3, buf.at[yp, lo]), (4, buf.at[y2, lo]), (5, buf.at[y2, hi])):
            wait_bytes(ref, yr_s.at[s0 + i])
    for swap in swaps:
        swap.wait_recv()

    def core_sum(h, i):
        xb = (x + 1 + i) % NX
        wait_bytes(prx.at[h, i], pr_s.at[NX * h + i])
        return pbuf[h, xb, :, c] + prx[h, i]

    def ship(h, i):
        xb = (x + 1 + i) % NX
        rxs[h, i] = core_sum(h, i).astype(BF)
        remote(rxs.at[h, i], rxr.at[h, i], xs_s.at[NX * h + i], xr_s.at[NX * h + i], dev_g(2 * xb + c)).start()

    for h in range(2):
        for i in range(NX):
            xb = (x + 1 + i) % NX

            @pl.loop(0, 4)
            def _(mt):
                rows = pl.ds(mt * 128, 128)
                early, late = fbuf[h, :part].reshape(part * HB, QH), fbuf[h, part:].reshape((LIVE - part) * HB, QH)
                term = jnp.dot(at1[xb, rows, :], early, preferred_element_type=F32)
                term = term + jnp.dot(at2[xb, rows, :], late, preferred_element_type=F32)
                pbuf[h, xb, pl.ds(mt * 2, 2)] = term.reshape(2, 2, TB, QH)

            remote(pbuf.at[h, xb, :, 1 - c], prx.at[h, i], ps_s.at[NX * h + i], pr_s.at[NX * h + i], core).start()
            if i > 0:
                ship(h, i - 1)

    for h in range(2):
        total = core_sum(h, NX - 1)
        for i in range(NX - 1):
            wait_bytes(rxr.at[h, i], xr_s.at[NX * h + i])
            total = total + rxr[h, i].astype(F32)
        rzs[h] = total.astype(BF)
        for i in range(1, NZ):
            zz = (z + i) % NZ
            remote(rzs.at[h, zz], rzr.at[h, z], sems.at[6 + h], sems.at[8 + h], dev_z(zz)).start()
        rzr[h, z] = rzs[h, z]
    for h in range(2):
        wait_bytes(rzs.at[h, pl.ds(0, NZ - 1)], sems.at[8 + h])
        final = rzr[h, 0].astype(F32)
        for zz in range(1, NZ):
            final = final + rzr[h, zz].astype(F32)
        out[:, h * QH : (h + 1) * QH] = final * (1.0 / math.sqrt(TB * TB * LIVE))

    wait_bytes(comb.at[pl.ds(0, NZ - 1)], cs_s.at[0])
    wait_bytes(comb.at[pl.ds(0, NX * NZ)], cs_s.at[1])
    wait_bytes(comb.at[pl.ds(0, (NX - 1) * NZ)], cs_s.at[2])
    for k in range(NZ):
        wait_bytes(txr[k].at[pl.ds(0, (NG - 1) * W)], out_s.at[k])
    wait_bytes(tc.at[pl.ds(0, NZ - 1)], sems.at[1])
    for k in range(NZ):
        wait_bytes(hxr[k].at[pl.ds(0, (NG - 1) * W)], out_s.at[NZ + k])
    wait_bytes(hc.at[pl.ds(0, NZ - 1)], sems.at[3])
    for swap in swaps:
        swap.wait_send()
    for i in range(6):
        wait_bytes(at1.at[y, lo], ys_s.at[i])
        wait_bytes(at2.at[y, lo], ys_s.at[6 + i])
    for h in range(2):
        wait_bytes(rzs.at[h, pl.ds(0, NZ - 1)], sems.at[6 + h])
        for i in range(NX - 1):
            wait_bytes(rxs.at[h, i], xs_s.at[NX * h + i])
        for i in range(NX):
            wait_bytes(prx.at[h, i], ps_s.at[NX * h + i])


def fused(cap, part, cid, *operands):
    vmem = pl.BlockSpec(memory_space=pltpu.VMEM)
    hbm = pl.BlockSpec(memory_space=pl.ANY)
    dma = pltpu.SemaphoreType.DMA
    return pl.pallas_call(
        functools.partial(kernel, cap, part),
        out_shape=jax.ShapeDtypeStruct((TB, QL), F32),
        in_specs=[vmem] * 5 + [hbm],
        out_specs=vmem,
        scratch_shapes=[
            pltpu.VMEM((16, 128), jnp.int32),
            pltpu.SMEM((16, 128), jnp.int32),
            pltpu.VMEM((W, TB, TB, QL), BF),
            pltpu.VMEM((TB, W, TB, QL), BF),
            pltpu.VMEM((RANKS, TB, 384), BF),
            pltpu.VMEM((HB, W * TB, QH), F32),
            pltpu.VMEM((2, TB, W, TB, QH), BF),
        ]
        + [pltpu.VMEM((NG * W, HB, QL), BF)] * NZ
        + [pltpu.VMEM((NG * W, TB, QH), BF)] * NZ
        + [
            pltpu.VMEM((NZ, cap, HB, QL), BF),
            pltpu.VMEM((NZ, cap, TB, QH), BF),
            pltpu.VMEM((NA, cap, HB, QL), BF),
            pltpu.VMEM((NZ - NA, cap, HB, QL), BF),
            pltpu.VMEM((NZ, cap, TB, QH), BF),
            pltpu.VMEM((NY, QL, part * HB), BF),
            pltpu.VMEM((NY, QL, (LIVE - part) * HB), BF),
            pltpu.VMEM((2, LIVE, HB, QH), BF),
            pltpu.VMEM((LIVE, HB, QH), BF),
            pltpu.VMEM((2, NX, NZ, 2, TB, QH), F32),
            pltpu.VMEM((2, NX, NZ, TB, QH), F32),
            pltpu.VMEM((2, NX - 1, NZ, TB, QH), BF),
            pltpu.VMEM((2, NX - 1, NZ, TB, QH), BF),
            pltpu.VMEM((2, NZ, TB, QH), BF),
            pltpu.VMEM((2, NZ, TB, QH), BF),
            dma((10,)),
            dma((NZ,)),
            dma((NZ,)),
            dma((NZ,)),
            dma((NZ,)),
            dma((12,)),
            dma((12,)),
            dma((3,)),
            dma((3,)),
            dma((4,)),
            dma((2 * NZ,)),
            dma((2 * NZ,)),
            dma((2 * NX,)),
            dma((2 * NX,)),
            dma((2 * NX,)),
            dma((2 * NX,)),
            dma((8,)),
        ],
        compiler_params=pltpu.CompilerParams(
            collective_id=cid, has_side_effects=True, vmem_limit_bytes=62 * 2**20
        ),
    )(*operands)


def per_device(three_index, occ_blocks, virt_blocks, tile_shift, tile_count, block_owner):
    plane_of = np.arange(RANKS) // 2 % NZ
    planes = np.arange(NZ)[:, None]
    early = np.isin((planes - plane_of) % NZ, OFF[:NA])
    chosen = np.concatenate([planes == plane_of, early]).astype(np.int32)
    tiles = jnp.sum(tile_count[None, :] * chosen, axis=1)
    is_plane = np.arange(2 * NZ) < NZ
    need = jnp.where(is_plane | (tiles >= SIZES[0][1]), 0, len(SIZES) - 1)
    for cap, _ in SIZES[:-1]:
        need = need + jnp.where(is_plane & (tiles > cap), 1, 0)
    return lax.switch(
        jnp.max(need),
        [functools.partial(fused, cap, part, 1 + i) for i, (cap, part) in enumerate(SIZES)],
        tile_count.reshape(1, RANKS),
        block_owner.reshape(1, RANKS),
        tile_shift,
        virt_blocks,
        occ_blocks,
        three_index,
    )


def solution(mesh):
    in_specs = (
        P("pair", None, None, "aux"),
        P("pair", None, None, None),
        P("pair", None, None, None),
        P(),
        P(),
        P(),
    )
    return jax.shard_map(per_device, mesh=mesh, in_specs=in_specs, out_specs=P("pair", "aux"), check_vma=False)
```
